32 devices in a mesh: dp: 8 (over y, x, core), tensor: 4 (over z).
Axes of the slice: x: 2, y: 2, z: 4, core: 2. Of those that a mesh axis runs over, the one named last changes fastest.
Arguments:
- tokens: bfloat16 [16384, 768], P('dp'), may hold values from -6 to 6
- lengths: int32 [16], P('dp'), may hold values from 256 to 1024
- cotangent: bfloat16 [16384, 768], P('dp'), may hold values from -6 to 6
- qkv_weight: bfloat16 [3, 768, 768], P(None, None, 'tensor'), may hold values from -0.21875 to 0.21875
- qv_bias: float32 [2, 768], P(None, 'tensor'), may hold values from -3 to 3
- out_weight: bfloat16 [768, 768], P('tensor'), may hold values from -0.875 to 0.875
- out_bias: float32 [768], replicated, may hold values from -3 to 3
- first_gain: float32 [768], replicated, may hold values from 0.5 to 1.5
- first_shift: float32 [768], replicated, may hold values from -2 to 2
- up_weight: bfloat16 [768, 3072], P(None, 'tensor'), may hold values from -0.21875 to 0.21875
- up_bias: float32 [3072], P('tensor'), may hold values from -3 to 3
- down_weight: bfloat16 [3072, 768], P('tensor'), may hold values from -0.15625 to 0.15625
- down_bias: float32 [768], replicated, may hold values from -3 to 3
- second_gain: float32 [768], replicated, may hold values from 0.5 to 1.5
- second_shift: float32 [768], replicated, may hold values from -2 to 2
Outputs:
- output: bfloat16 [16384, 768], P('dp')
- grad_tokens: float32 [16384, 768], P('dp', 'tensor')
- grad_qkv_weight: float32 [3, 768, 768], P(None, None, 'tensor')
- grad_qv_bias: float32 [2, 768], P(None, 'tensor')
- grad_out_weight: float32 [768, 768], P('tensor')
- grad_out_bias: float32 [768], replicated
- grad_first_gain: float32 [768], replicated
- grad_first_shift: float32 [768], replicated
- grad_up_weight: float32 [768, 3072], P(None, 'tensor')
- grad_up_bias: float32 [3072], P('tensor')
- grad_down_weight: float32 [3072, 768], P('tensor')
- grad_down_bias: float32 [768], replicated
- grad_second_gain: float32 [768], replicated
- grad_second_shift: float32 [768], replicated
The draws below stay inside these ranges and needn't reach their ends.
All inputs are finite; a program needn't handle non-finite values.
Results may differ from the reference program's by a relative error of at most 0.014.
The reference program's roundings to bfloat16 on the way count: a program that leaves them out, or rounds other values in their place, can miss the bound.
Values sent between devices are 32-bit elements; how exact they have to be, the bound alone decides.
No kernel may reach another device: no remote copies, remote signals or barrier semaphores. Data moves between devices by JAX's collectives and lax.ppermute only.
A program may use at most 192 MiB of HBM per device.

```python
import jax
import jax.numpy as jnp
from jax import lax

D = 768
HEADS = 12
HD = 64
FF = 3072
LEN = 1024
SEQS = 16
TOKENS = 16384


def with_ends(values, rng, least, largest):
    longest = values.shape.index(max(values.shape))
    spots = []
    for shift in (0, 1):
        where = [jax.random.randint(jax.random.fold_in(rng, axis), (), 0, length) for axis, length in enumerate(values.shape)]
        where[longest] = (where[longest] + shift) % values.shape[longest]
        spots.append(tuple(where))
    return values.at[spots[0]].set(least).at[spots[1]].set(largest)


def levels(rng, dims, shards, smallest, high):
    def one(dim, shards_of):
        heights = jax.random.uniform(jax.random.fold_in(jax.random.fold_in(rng, 6), dim), (shards_of,), jnp.float32, smallest / len(shards), high / len(shards))
        return jnp.repeat(jnp.exp(heights), dims[dim] // shards_of).reshape((-1,) + (1,) * (len(dims) - dim - 1))

    level = one(*shards[0])
    for cut in shards[1:]:
        level = level * one(*cut)
    return level


def gaussian(stream_key, extent, deviation, limit, split=(), kind=jnp.bfloat16):
    values = deviation * jax.random.normal(stream_key, extent, jnp.float32)
    if split:
        values = values * levels(stream_key, extent, split, -0.22, 0.18)
    return jnp.clip(values, -limit, limit).astype(kind)


def setup_inputs(seed: int = 0) -> dict:
    splits = jax.random.split(jax.random.key(seed), 16)
    tokens = gaussian(splits[0], (TOKENS, D), 1.0, 6.0, ((0, 8),))
    lengths = with_ends(jax.random.randint(splits[1], (SEQS,), LEN // 4, LEN + 1), jax.random.fold_in(splits[1], 1), LEN // 4, LEN).astype(jnp.int32)
    cotangent = gaussian(splits[2], (TOKENS, D), 1.0, 6.0, ((0, 8),))
    qkv_weight = gaussian(splits[3], (3, D, D), D ** -0.5, 0.21875, ((2, 4),))
    qv_bias = gaussian(splits[4], (2, D), 0.5, 3.0, ((1, 4),), jnp.float32)
    out_weight = gaussian(splits[5], (D, D), (D // 16) ** -0.5, 0.875, ((0, 4),))
    out_bias = gaussian(splits[6], (D,), 0.5, 3.0, (), jnp.float32)
    first_gain = jnp.clip(1.0 + 0.1 * jax.random.normal(splits[7], (D,), jnp.float32), 0.5, 1.5)
    first_shift = gaussian(splits[8], (D,), 0.3, 2.0, (), jnp.float32)
    up_weight = gaussian(splits[9], (D, FF), D ** -0.5, 0.21875, ((1, 4),))
    up_bias = gaussian(splits[10], (FF,), 0.5, 3.0, ((0, 4),), jnp.float32)
    down_weight = gaussian(splits[11], (FF, D), (FF // 2) ** -0.5, 0.15625, ((0, 4),))
    down_bias = gaussian(splits[12], (D,), 0.5, 3.0, (), jnp.float32)
    second_gain = jnp.clip(1.0 + 0.1 * jax.random.normal(splits[13], (D,), jnp.float32), 0.5, 1.5)
    second_shift = gaussian(splits[14], (D,), 0.3, 2.0, (), jnp.float32)
    return dict(tokens=tokens, lengths=lengths, cotangent=cotangent, qkv_weight=qkv_weight, qv_bias=qv_bias, out_weight=out_weight, out_bias=out_bias, first_gain=first_gain, first_shift=first_shift, up_weight=up_weight, up_bias=up_bias, down_weight=down_weight, down_bias=down_bias, second_gain=second_gain, second_shift=second_shift)


EPS = 1e-05
MASKED = -1000000000.0
HIGH = lax.Precision.HIGHEST

@jax.custom_vjp
def low(v):
    return lax.optimization_barrier(v.astype(jnp.bfloat16)).astype(jnp.float32)

@jax.custom_vjp
def low_back(v):
    return v

def low_keep(v):
    return (low(v), None)

def low_pass(kept, grad):
    return (grad,)

def back_keep(v):
    return (v, None)

def back_low(kept, grad):
    return (low(grad),)
low.defvjp(low_keep, low_pass)
low_back.defvjp(back_keep, back_low)

def layer_norm(hidden, gain, shift):
    center = hidden - lax.optimization_barrier(jnp.mean(hidden, -1, keepdims=True))
    spread = lax.optimization_barrier(jnp.mean(center * center, -1, keepdims=True))
    return center * lax.rsqrt(spread + EPS) * gain + shift

def matmul(left, right):
    return jnp.dot(left, right, precision=HIGH)

def one_sequence(weights, inputs, length):
    qkv_weight, qv_bias, out_weight, out_bias, first_gain, first_shift, up_weight, up_bias, down_weight, down_bias, second_gain, second_shift = weights
    seq_len = inputs.shape[0]
    shape_heads = (seq_len, HEADS, HD)
    scale = HD ** (-0.5)
    queries = low_back(low(matmul(inputs, qkv_weight[0]) + qv_bias[0])).reshape(shape_heads)
    keys_low = low_back(low(matmul(inputs, qkv_weight[1]))).reshape(shape_heads)
    values_low = low_back(low(matmul(inputs, qkv_weight[2]) + qv_bias[1])).reshape(shape_heads)
    scores = jnp.einsum('qhd,khd->hqk', queries, keys_low, precision=HIGH) * scale
    valid = jnp.arange(seq_len, dtype=jnp.int32) < length
    scores = low_back(jnp.where(valid[None, None, :], scores, MASKED))
    probs = low(jax.nn.softmax(scores, axis=-1))
    mixed = jnp.einsum('hqk,khd->qhd', probs, values_low, precision=HIGH).reshape(seq_len, D)
    mixed = low_back(low(mixed))
    attended = low_back(matmul(mixed, out_weight) + out_bias)
    normed = layer_norm(inputs + attended, first_gain, first_shift)
    hidden = low_back(matmul(low(normed), up_weight) + up_bias)
    active = low(jax.nn.gelu(hidden, approximate=False))
    branch = low_back(matmul(active, down_weight) + down_bias)
    return layer_norm(normed + branch, second_gain, second_shift)

def reference(tokens, lengths, cotangent, qkv_weight, qv_bias, out_weight, out_bias, first_gain, first_shift, up_weight, up_bias, down_weight, down_bias, second_gain, second_shift):
    params = (qkv_weight, qv_bias, out_weight, out_bias, first_gain, first_shift, up_weight, up_bias, down_weight, down_bias, second_gain, second_shift)
    params = tuple((item.astype(jnp.float32) for item in params))
    whole = tokens.astype(jnp.float32).reshape(SEQS, LEN, D)

    def forward(inputs, weights):
        step = jax.checkpoint(lambda pair: one_sequence(weights, pair[0], pair[1]))
        return lax.map(step, (inputs, lengths))
    result, pullback = jax.vjp(forward, whole, params)
    grad_inputs, grads = pullback(cotangent.astype(jnp.float32).reshape(SEQS, LEN, D))
    return (result.reshape(TOKENS, D).astype(jnp.bfloat16), grad_inputs.reshape(TOKENS, D), grads[0], grads[1], grads[2], grads[3], grads[4], grads[5], grads[6], grads[7], grads[8], grads[9], grads[10], grads[11])
```

```python
import jax
import jax.numpy as jnp
from jax import lax
from jax.experimental import pallas as pl
from jax.experimental.pallas import tpu as pltpu
from jax.sharding import PartitionSpec as P

HD = 64
EPS = 1e-05
MASKED = -1000000000.0
BITS = 3
INNER = 1 << BITS
F32 = jnp.float32
BF16 = jnp.bfloat16


def layer_norm(hidden, gain, shift):
    center = hidden - jnp.mean(hidden, -1, keepdims=True)
    spread = jnp.mean(center * center, -1, keepdims=True)
    return center * lax.rsqrt(spread + EPS) * gain + shift


def exact_gelu(inputs):
    return jax.nn.gelu(inputs, approximate=False)


def nn(left, right):
    return lax.dot_general(left, right, (((1,), (0,)), ((), ())), preferred_element_type=F32)


def nt(left, right):
    return lax.dot_general(left, right, (((1,), (1,)), ((), ())), preferred_element_type=F32)


def tn(left, right):
    return lax.dot_general(left, right, (((0,), (0,)), ((), ())), preferred_element_type=F32)


def flip(x, bit):
    size = lax.axis_size("dp")
    return lax.ppermute(x, "dp", [(i, i ^ (1 << bit)) for i in range(size)])


def from_next(x, step):
    size = lax.axis_size("tensor")
    return lax.ppermute(x, "tensor", [((i + step) % size, i) for i in range(size)])


def to_next(x, step):
    size = lax.axis_size("tensor")
    return lax.ppermute(x, "tensor", [(i, (i + step) % size) for i in range(size)])


ORDERS = ((1, 2), (2, 1))


def unit(lengths):
    return jnp.where(lengths[0] > 0, 1.0, 0.0).astype(F32)


def gather_pieces(piece):
    piece = lax.optimization_barrier(piece)
    places = [piece] + [from_next(piece, step) for step in (1, 2, 3)]
    halves = []
    for half, order in enumerate(ORDERS):
        held = jnp.concatenate(places[2 * half : 2 * half + 2], 0)
        for bit in order:
            held = jnp.concatenate([held, flip(held, bit)], 0)
        halves.append(lax.optimization_barrier((held, flip(held, 0))))
    return halves


def scatter_sums(halves):
    places = []
    for (own, other), order in zip(halves, ORDERS):
        held = own + flip(other, 0)
        for bit in reversed(order):
            count = held.shape[0] // 2
            held = held[:count] + flip(held[count:], bit)
        count = held.shape[0] // 2
        places += [held[:count], held[count:]]
    total = places[0]
    for step in (1, 2, 3):
        total = total + to_next(places[step], step)
    bit = BITS
    while (1 << bit) < lax.axis_size("dp"):
        total = total + flip(total, bit)
        bit += 1
    return total


def gather_in_order(piece, order):
    held = piece[None]
    for bit in (*order, 0):
        held = jnp.concatenate([held, flip(held, bit)], 0)
    me = lax.axis_index("dp") % INNER
    blocks = []
    for index in range(INNER):
        apart = me ^ index
        place = sum(((apart >> bit) & 1) << at for at, bit in enumerate((*order, 0)))
        blocks.append(lax.dynamic_index_in_dim(held, place, 0))
    return jnp.concatenate(blocks, 0)


def sum_everywhere(x):
    for axis in ("dp", "tensor"):
        size = lax.axis_size(axis)
        step = 1
        while step < size:
            x = x + lax.ppermute(x, axis, [(i, i ^ step) for i in range(size)])
            step *= 2
    return x


CHUNK = 256


def lane_masks(width):
    lane = lax.broadcasted_iota(jnp.int32, (1, width), 1)
    return [lane < HD, lane >= HD]


def keep(mask, x):
    return jnp.where(mask, x, jnp.zeros_like(x))


def forward_kernel(length_ref, q_ref, k_ref, v_ref, mixed_ref, lse_ref):
    keys = k_ref.shape[0]
    queries = q_ref.shape[0]
    valid = lax.broadcasted_iota(jnp.int32, (keys, 1), 0) < length_ref[0]
    masks = lane_masks(q_ref.shape[1])
    turned = v_ref[...].T
    for start in range(0, queries, CHUNK):
        rows = pl.ds(start, CHUNK)
        parts = []
        for head in range(2):
            scores = nt(k_ref[...], keep(masks[head], q_ref[rows, :]))
            scores = jnp.where(valid, scores, MASKED)
            highest = jnp.max(scores, 0, keepdims=True)
            expo = jnp.exp(scores - highest)
            totals = jnp.sum(expo, 0, keepdims=True)
            probs = (expo * (1.0 / totals)).astype(BF16)
            parts.append(nn(turned[head * HD : (head + 1) * HD, :], probs))
            lse_ref[0, head : head + 1, rows] = highest + jnp.log(totals)
        mixed_ref[rows, :] = jnp.concatenate(parts, 0).T.astype(BF16)


def backward_kernel(length_ref, q_ref, k_ref, v_ref, dm_ref, lse_ref, dq_ref, dk_ref, dv_ref, dk_sum, dv_sum):
    keys = k_ref.shape[0]
    queries = q_ref.shape[0]
    valid = lax.broadcasted_iota(jnp.int32, (keys, 1), 0) < length_ref[0]
    masks = lane_masks(q_ref.shape[1])
    turned = k_ref[...].T
    for start in range(0, queries, CHUNK):
        rows = pl.ds(start, CHUNK)
        parts = []
        for head in range(2):
            query = keep(masks[head], q_ref[rows, :])
            d_mixed = keep(masks[head], dm_ref[rows, :])
            scores = jnp.where(valid, nt(k_ref[...], query), MASKED)
            probs = jnp.exp(scores - lse_ref[0, head : head + 1, rows])
            d_values = nn(probs.astype(BF16), d_mixed)
            d_probs = nt(v_ref[...], d_mixed)
            row_dot = jnp.sum(d_probs * probs, 0, keepdims=True)
            d_scores = (probs * (d_probs - row_dot)).astype(BF16)
            d_keys = nn(d_scores, query)
            parts.append(nn(turned[head * HD : (head + 1) * HD, :], d_scores))
            if start == 0 and head == 0:
                dk_sum[...] = d_keys
                dv_sum[...] = d_values
            else:
                dk_sum[...] += d_keys
                dv_sum[...] += d_values
        dq_ref[rows, :] = (jnp.concatenate(parts, 0).T * HD ** (-0.5)).astype(BF16)
    dk_ref[...] = dk_sum[...].astype(BF16)
    dv_ref[...] = dv_sum[...].astype(BF16)


def attention_forward(length, queries, keys, values):
    count, width = queries.shape
    pairs = width // (2 * HD)
    columns = lambda rows: pl.BlockSpec((rows, 2 * HD), lambda j: (0, j))
    work = count * keys.shape[0] * width
    return pl.pallas_call(
        forward_kernel,
        grid=(pairs,),
        in_specs=[
            pl.BlockSpec(memory_space=pltpu.SMEM),
            columns(count),
            columns(keys.shape[0]),
            columns(keys.shape[0]),
        ],
        out_specs=[columns(count), pl.BlockSpec((1, 2, count), lambda j: (j, 0, 0))],
        out_shape=[
            jax.ShapeDtypeStruct((count, width), BF16),
            jax.ShapeDtypeStruct((pairs, 2, count), F32),
        ],
        compiler_params=pltpu.CompilerParams(vmem_limit_bytes=48 * 2**20),
        cost_estimate=pl.CostEstimate(flops=8 * work, bytes_accessed=4 * 2**20, transcendentals=work // HD),
    )(length, queries, keys, values)


def attention_backward(length, queries, keys, values, d_mixed, lse):
    count, width = queries.shape
    pairs = width // (2 * HD)
    long = keys.shape[0]
    columns = lambda rows: pl.BlockSpec((rows, 2 * HD), lambda j: (0, j))
    work = count * long * width
    return pl.pallas_call(
        backward_kernel,
        grid=(pairs,),
        in_specs=[
            pl.BlockSpec(memory_space=pltpu.SMEM),
            columns(count),
            columns(long),
            columns(long),
            columns(count),
            pl.BlockSpec((1, 2, count), lambda j: (j, 0, 0)),
        ],
        out_specs=[columns(count), columns(long), columns(long)],
        out_shape=[
            jax.ShapeDtypeStruct((count, width), BF16),
            jax.ShapeDtypeStruct((long, width), BF16),
            jax.ShapeDtypeStruct((long, width), BF16),
        ],
        scratch_shapes=[pltpu.VMEM((long, 2 * HD), F32)] * 2,
        compiler_params=pltpu.CompilerParams(vmem_limit_bytes=48 * 2**20),
        cost_estimate=pl.CostEstimate(flops=20 * work, bytes_accessed=8 * 2**20, transcendentals=work // HD),
    )(length, queries, keys, values, d_mixed, lse)


def share_input_grads(part):
    seq, width = part.shape
    piece = width // 4
    place = lax.axis_index("tensor")
    flipped = place >= 2
    quarters = [part[:, i * piece : (i + 1) * piece] for i in range(4)]
    near = [jnp.where(flipped, quarters[3 - i], quarters[i]) for i in range(4)]
    outer = (place == 0) | (place == 3)
    swap = [(0, 1), (1, 0), (2, 3), (3, 2)]
    inward = [(0, 1), (3, 2)]
    across = [(1, 2), (2, 1)]
    outward = [(2, 3), (1, 0)]
    first = lax.ppermute(jnp.where(outer, near[3], near[0]), "tensor", swap)
    far = lax.ppermute(near[3] + first, "tensor", across)
    second = lax.ppermute(near[2], "tensor", inward)
    third = lax.ppermute(near[1], "tensor", inward)
    middle = lax.ppermute(near[2] + second, "tensor", across)
    last = lax.ppermute(far, "tensor", outward)
    mine = jnp.where(outer, near[0] + first, near[1] + third)
    theirs = jnp.where(outer, last, middle)
    return jnp.concatenate([jnp.where(flipped, theirs, mine), jnp.where(flipped, mine, theirs)], 0)


def head_rows(array, heads):
    cols = array.shape[1]
    return array.reshape(heads, INNER, HD // INNER, cols).transpose(1, 0, 2, 3)


def on_device(
    tokens,
    lengths,
    cotangent,
    qkv_weight,
    qv_bias,
    out_weight,
    out_bias,
    first_gain,
    first_shift,
    up_weight,
    up_bias,
    down_weight,
    down_bias,
    second_gain,
    second_shift,
):
    rows, width = tokens.shape
    seq = rows // lengths.shape[0]
    columns = qkv_weight.shape[2]
    heads = columns // HD
    units = up_weight.shape[1]
    share = rows // 4
    sub = HD // INNER
    place = lax.axis_index("tensor")
    me = lax.axis_index("dp") % INNER
    one = unit(lengths)

    turned = jnp.concatenate([qkv_weight.transpose(0, 2, 1), out_weight[None]], 0)
    turned = turned.reshape(4, heads, INNER, sub, width)
    attn_piece = lax.dynamic_index_in_dim(turned, me, 2, keepdims=False).reshape(-1, width).astype(F32) * one
    count = units // INNER
    up_piece = lax.dynamic_slice_in_dim(up_weight.T, me * count, count, 0).astype(F32) * one
    down_piece = lax.dynamic_slice_in_dim(down_weight, me * count, count, 0).astype(F32) * one
    qv_piece = lax.dynamic_index_in_dim(qv_bias.reshape(2 * heads, INNER, sub), me, 1, keepdims=False)
    bias_piece = jnp.zeros((8, 128), F32)
    bias_piece = bias_piece.at[0, :count].set(lax.dynamic_slice_in_dim(up_bias, me * count, count, 0))
    bias_piece = bias_piece.at[1, : 2 * heads * sub].set(qv_piece.reshape(-1))

    bias_halves = gather_pieces(bias_piece)
    attn_halves = gather_pieces(attn_piece)
    up_halves = gather_pieces(up_piece)
    down_halves = gather_pieces(down_piece)

    def heads_together(own, other, kinds, trail):
        both = jnp.stack([own, other]).reshape((2, 2, 2, 2, kinds, heads, sub) + trail)
        both = both.transpose((4, 3, 5, 0, 1, 2, 6) + tuple(range(7, 7 + len(trail))))
        return both.reshape((kinds, 2 * heads * HD) + trail)

    def heads_apart(array, kinds, trail):
        both = array.reshape((kinds, 2, 2, heads, 2, 2, 2, sub) + trail)
        both = both.transpose((1, 4, 5, 6, 2, 0, 3, 7) + tuple(range(8, 8 + len(trail))))
        flat = both.reshape((2, 2, 4 * 2 * kinds * heads * sub) + trail)
        return [(flat[half, 0], flat[half, 1]) for half in range(2)]

    attn_full = jnp.concatenate(
        [(heads_together(own, other, 4, (width,)) * one).astype(BF16) for own, other in attn_halves], 1
    )
    q_rows, k_rows, v_rows, out_rows = attn_full
    qv_full = jnp.concatenate(
        [
            heads_together(
                own.reshape(8, 8, 128)[:, 1, : 2 * heads * sub],
                other.reshape(8, 8, 128)[:, 1, : 2 * heads * sub],
                2,
                (),
            )
            for own, other in bias_halves
        ],
        1,
    )
    up_bias_full = jnp.concatenate(
        [part.reshape(8, 8, 128)[:, 0, :count].reshape(-1) for pair in bias_halves for part in pair]
    )
    up_full = jnp.concatenate([part for pair in up_halves for part in pair], 0) * one
    down_full = jnp.concatenate([part for pair in down_halves for part in pair], 0) * one

    up_full = up_full.astype(BF16)
    down_full = down_full.astype(BF16)

    which = place // 2
    length = lax.dynamic_slice_in_dim(lengths, which, 1, 0)
    seq_tokens = lax.dynamic_slice_in_dim(tokens, which * seq, seq, 0)
    own_tokens = lax.dynamic_slice_in_dim(tokens, place * share, share, 0)
    own_cotangent = lax.dynamic_slice_in_dim(cotangent, place * share, share, 0)
    queries = (nt(own_tokens, q_rows) + qv_full[0]).astype(BF16) * jnp.asarray(HD ** (-0.5), BF16)
    keys = nt(seq_tokens, k_rows).astype(BF16)
    values = (nt(seq_tokens, v_rows) + qv_full[1]).astype(BF16)
    mixed, lse = attention_forward(length, queries, keys, values)
    attended = nn(mixed, out_rows) + out_bias
    first = own_tokens.astype(F32) + attended
    normed, first_back = jax.vjp(layer_norm, first, first_gain, first_shift)
    normed_low = normed.astype(BF16)
    hidden = nt(normed_low, up_full) + up_bias_full
    active_full, gelu_back = jax.vjp(exact_gelu, hidden)
    active = active_full.astype(BF16)
    second = normed + (nn(active, down_full) + down_bias)
    result, second_back = jax.vjp(layer_norm, second, second_gain, second_shift)
    output = (lax.all_gather(result, "tensor", axis=0, tiled=True) * one).astype(BF16)

    d_second, grad_second_gain, grad_second_shift = second_back(own_cotangent.astype(F32))
    d_branch = d_second.astype(BF16)
    grad_down_bias = jnp.sum(d_branch.astype(F32), 0)
    d_active = nt(d_branch, down_full)
    d_hidden = gelu_back(d_active)[0].astype(BF16)

    def unit_grads(left, right):
        parts = [tn(left[:, i * units : (i + 1) * units], right) for i in range(4)]
        return [(parts[0], parts[1]), (parts[2], parts[3])]

    down_sums = scatter_sums(unit_grads(active, d_branch))
    up_sums = scatter_sums(unit_grads(d_hidden, normed_low))
    grad_up_bias = jnp.sum(d_hidden.astype(F32), 0)
    d_normed = nn(d_hidden, up_full) + d_second
    d_first, grad_first_gain, grad_first_shift = first_back(d_normed)
    d_attended = d_first.astype(BF16)
    grad_out_rows = tn(mixed, d_attended)
    grad_out_bias = jnp.sum(d_attended.astype(F32), 0)
    d_mixed = nt(d_attended, out_rows).astype(BF16)
    d_queries, d_keys, d_values = attention_backward(length, queries, keys, values, d_mixed, lse)

    input_part = nn(d_keys, k_rows) + nn(d_values, v_rows)
    own_part = nn(d_queries, q_rows) + d_first
    offset = (place % 2) * share
    input_part = lax.dynamic_update_slice_in_dim(
        input_part, lax.dynamic_slice_in_dim(input_part, offset, share, 0) + own_part, offset, 0
    )
    grad_tokens = share_input_grads(input_part)

    attn_grads = jnp.stack(
        [tn(d_queries, own_tokens), tn(d_keys, seq_tokens), tn(d_values, seq_tokens), grad_out_rows]
    )
    attn_sums = scatter_sums(heads_apart(attn_grads, 4, (width,)))
    qv_sums = heads_apart(
        jnp.stack([jnp.sum(d_queries.astype(F32), 0), jnp.sum(d_values.astype(F32), 0)]), 2, ()
    )
    up_bias_parts = grad_up_bias.reshape(2, 2, 8, count)
    bias_parts = []
    for half in range(2):
        pair = []
        for core in range(2):
            block = jnp.zeros((8, 8, 128), F32)
            block = block.at[:, 0, :count].set(up_bias_parts[half, core])
            block = block.at[:, 1, : 2 * heads * sub].set(qv_sums[half][core].reshape(8, -1))
            pair.append(block.reshape(64, 128))
        bias_parts.append(tuple(pair))
    bias_sums = scatter_sums(bias_parts)

    bias_all = gather_in_order(bias_sums, (1, 2))
    down_all = gather_in_order(down_sums, (1, 2))
    up_all = gather_in_order(up_sums, (2, 1))
    attn_all = gather_in_order(attn_sums, (1, 2))
    attn_all = attn_all.reshape(INNER, 4, heads, sub, width).transpose(1, 2, 0, 3, 4)
    attn_all = attn_all.reshape(4, columns, width)
    qv_all = bias_all[:, 1, : 2 * heads * sub].reshape(INNER, 2, heads, sub)
    small = sum_everywhere(
        jnp.stack(
            [
                grad_out_bias,
                grad_first_gain,
                grad_first_shift,
                grad_down_bias,
                grad_second_gain,
                grad_second_shift,
            ]
        )
    )
    return (
        output,
        grad_tokens,
        attn_all[:3].transpose(0, 2, 1),
        qv_all.transpose(1, 2, 0, 3).reshape(2, columns),
        attn_all[3],
        small[0],
        small[1],
        small[2],
        up_all.reshape(units, width).T,
        bias_all[:, 0, :count].reshape(-1),
        down_all.reshape(units, width),
        small[3],
        small[4],
        small[5],
    )


def solution(mesh):
    placed = (
        P("dp", None),
        P("dp"),
        P("dp", None),
        P(None, None, "tensor"),
        P(None, "tensor"),
        P("tensor", None),
        P(),
        P(),
        P(),
        P(None, "tensor"),
        P("tensor"),
        P("tensor", None),
        P(),
        P(),
        P(),
    )
    return jax.shard_map(
        on_device,
        mesh=mesh,
        in_specs=placed,
        out_specs=(
            P("dp", None),
            P("dp", "tensor"),
            P(None, None, "tensor"),
            P(None, "tensor"),
            P("tensor", None),
            P(),
            P(),
            P(),
            P(None, "tensor"),
            P("tensor"),
            P("tensor", None),
            P(),
            P(),
            P(),
        ),
        check_vma=False,
    )
```

```python
import jax
import jax.numpy as jnp
from jax import lax
from jax.experimental import pallas as pl
from jax.experimental.pallas import tpu as pltpu
from jax.sharding import PartitionSpec as P

HD = 64
EPS = 1e-05
MASKED = -1000000000.0
BITS = 3
INNER = 1 << BITS
F32 = jnp.float32
BF16 = jnp.bfloat16


def layer_norm(hidden, gain, shift):
    center = hidden - jnp.mean(hidden, -1, keepdims=True)
    spread = jnp.mean(center * center, -1, keepdims=True)
    return center * lax.rsqrt(spread + EPS) * gain + shift


def exact_gelu(inputs):
    return jax.nn.gelu(inputs, approximate=False)


def nn(left, right):
    return lax.dot_general(left, right, (((1,), (0,)), ((), ())), preferred_element_type=F32)


def nt(left, right):
    return lax.dot_general(left, right, (((1,), (1,)), ((), ())), preferred_element_type=F32)


def tn(left, right):
    return lax.dot_general(left, right, (((0,), (0,)), ((), ())), preferred_element_type=F32)


APART = [c | (x << 1) | (y << 2) for c in (0, 1) for y in (0, 1) for x in (0, 1)]


def unit(lengths):
    return jnp.where(lengths[0] > 0, 1.0, 0.0).astype(F32)


def after(x, *others):
    return lax.optimization_barrier((x, others))[0]


def flip(x, bit):
    size = lax.axis_size("dp")
    return lax.ppermute(x, "dp", [(i, i ^ (1 << bit)) for i in range(size)])


def from_next(x, step):
    size = lax.axis_size("tensor")
    return lax.ppermute(x, "tensor", [((i + step) % size, i) for i in range(size)])


def to_next(x, step):
    size = lax.axis_size("tensor")
    return lax.ppermute(x, "tensor", [(i, (i + step) % size) for i in range(size)])


def relative(x, axis):
    me = lax.axis_index("dp") % INNER
    return jnp.concatenate([lax.dynamic_slice_in_dim(x, me ^ apart, 1, axis) for apart in APART], axis)


def apart_of(step):
    return (step // 4) | ((step % 2) << 1) | (((step // 2) % 2) << 2)


def relative_kernel(me_ref, *refs):
    count = len(refs) // 2
    for source, target in zip(refs[:count], refs[count:]):
        target[...] = source[...]


def relative_blocks(me, *arrays):
    def spec(array, index):
        lead = array.ndim - 3
        block = array.shape[:lead] + (1,) + array.shape[lead + 1 :]
        return pl.BlockSpec(block, lambda k, me_ref: (0,) * lead + (index(k, me_ref), 0, 0))

    return pl.pallas_call(
        relative_kernel,
        grid_spec=pltpu.PrefetchScalarGridSpec(
            num_scalar_prefetch=1,
            grid=(INNER,),
            in_specs=[spec(array, lambda k, me_ref: me_ref[0] ^ apart_of(k)) for array in arrays],
            out_specs=[spec(array, lambda k, me_ref: k) for array in arrays],
        ),
        out_shape=[jax.ShapeDtypeStruct(array.shape, array.dtype) for array in arrays],
        compiler_params=pltpu.CompilerParams(vmem_limit_bytes=48 * 2**20),
    )(me, *arrays)


def units_kernel(near_ref, a_ref, a_far_ref, b_ref, b_far_ref, out_ref):
    step = pl.program_id(0)
    half = a_ref.shape[2]
    out_ref[0, 0] = near_ref[0]

    @pl.when(step < 2)
    def _():
        out_ref[0, 1:, :half] = a_ref[0].astype(BF16)

    @pl.when(step >= 2)
    def _():
        out_ref[0, 1:, :half] = a_far_ref[0].astype(BF16)

    @pl.when(step % 2 == 0)
    def _():
        out_ref[0, 1:, half:] = b_ref[0].astype(BF16)

    @pl.when(step % 2 == 1)
    def _():
        out_ref[0, 1:, half:] = b_far_ref[0].astype(BF16)


def units_together(near, core, parts):
    count, width = near.shape[1:]
    half = count // 2
    by_x = pl.BlockSpec((1, 3, half, width), lambda k: (k % 2, 0, 0, 0))
    by_y = pl.BlockSpec((1, 3, half, width), lambda k: (k // 2, 0, 0, 0))
    full = pl.pallas_call(
        units_kernel,
        grid=(4,),
        in_specs=[pl.BlockSpec((1, count, width), lambda k: (4 * core + k, 0, 0)), by_x, by_x, by_y, by_y],
        out_specs=pl.BlockSpec((1, 4, count, width), lambda k: (k, 0, 0, 0)),
        out_shape=jax.ShapeDtypeStruct((4, 4, count, width), BF16),
        compiler_params=pltpu.CompilerParams(vmem_limit_bytes=48 * 2**20),
    )(near, *parts)
    return full.reshape(16 * count, width)


def gather_places(piece):
    return jnp.stack([from_next(piece, step) for step in (1, 2, 3)])


def gather_halves(piece):
    half = piece.shape[0] // 2
    places = [from_next(piece, step) for step in (1, 2, 3)]
    return [jnp.stack([place[:half] for place in places]), jnp.stack([place[half:] for place in places])]


def gather_first(held, route, recv=lambda x: x):
    return jnp.stack([held, recv(flip(held, 2 if route else 1))])


def gather_second(held, route, recv=lambda x: x):
    if route:
        return jnp.stack([held, recv(flip(held, 1))], 1)
    return jnp.stack([held, recv(flip(held, 2))])


def scatter_first(held, route, recv=lambda x: x):
    if route:
        got = recv(flip(held[:, 1], 1))
        return held[0, 0] + got[0], held[1, 0] + got[1]
    got = recv(flip(held[1], 2))
    return held[0, 0] + got[0], held[0, 1] + got[1]


def scatter_second(parts, route, recv=lambda x: x):
    return parts[0] + recv(flip(parts[1], 2 if route else 1))


def scatter_places(places, recv=lambda x: x):
    total = places[0]
    for step in (1, 2, 3):
        total = total + recv(to_next(places[step], step))
    bit = BITS
    while (1 << bit) < lax.axis_size("dp"):
        total = total + flip(total, bit)
        bit += 1
    return total


def gather_in_order(piece, order):
    held = piece[None]
    for bit in (*order, 0):
        held = jnp.concatenate([held, flip(held, bit)], 0)
    me = lax.axis_index("dp") % INNER
    blocks = []
    for index in range(INNER):
        apart = me ^ index
        place = sum(((apart >> bit) & 1) << at for at, bit in enumerate((*order, 0)))
        blocks.append(lax.dynamic_index_in_dim(held, place, 0))
    return jnp.concatenate(blocks, 0)


def sum_everywhere(x, others):
    others = list(others)
    for axis in ("dp", "tensor"):
        size = lax.axis_size(axis)
        step = 1
        while step < size:
            got = lax.ppermute(x, axis, [(i, i ^ step) for i in range(size)])
            x = x + (after(got, others.pop(0)) if others else got)
            step *= 2
    return x


CHUNK = 256


def lane_masks(width):
    lane = lax.broadcasted_iota(jnp.int32, (1, width), 1)
    return [(lane >= start) & (lane < start + HD) for start in range(0, width, HD)]


def keep(mask, x):
    return jnp.where(mask, x, jnp.zeros_like(x))


def softmax_turned(keys, query, valid):
    scores = jnp.where(valid, nt(keys, query), MASKED)
    expo = jnp.exp(scores - jnp.max(scores, 0, keepdims=True))
    return expo * (1.0 / jnp.sum(expo, 0, keepdims=True))


def forward_kernel(me_ref, lengths_ref, q_ref, k_ref, v_ref, mixed_ref):
    keys = k_ref.shape[0]
    queries = q_ref.shape[0]
    valid = lax.broadcasted_iota(jnp.int32, (keys, 1), 0) < lengths_ref[pl.program_id(0)]
    masks = lane_masks(q_ref.shape[1])
    turned = v_ref[...].T
    sub = HD // INNER
    spots = []
    for block in range(INNER):
        apart = me_ref[0] ^ block
        spots.append((apart & 1) * 4 + (apart >> 2) * 2 + ((apart >> 1) & 1))
    for start in range(0, queries, CHUNK):
        rows = pl.ds(start, CHUNK)
        for head, mask in enumerate(masks):
            probs = softmax_turned(k_ref[...], keep(mask, q_ref[rows, :]), valid).astype(BF16)
            part = nn(turned[head * HD : (head + 1) * HD, :], probs).astype(BF16).astype(F32)
            for block, spot in enumerate(spots):
                at = pl.multiple_of(head * HD + spot * sub, sub)
                mixed_ref[pl.ds(at, sub), rows] = part[block * sub : (block + 1) * sub, :]


def backward_kernel(last, scalars_ref, *refs):
    q_ref, k_ref, v_ref, dm_ref, mixed_ref, wq_ref, wk_ref, wv_ref, own_ref, seq_ref, da_ref = refs[:11]
    given, refs = (refs[11:13], refs[13:]) if last else (refs[11:12], refs[12:])
    near_ref, far_ref, sums_ref, own_part_ref, seq_part_ref, dk_sum, dv_sum, dq_all, dq_turned = refs
    keys = k_ref.shape[0]
    queries = q_ref.shape[0]
    step = pl.program_id(0)
    valid = lax.broadcasted_iota(jnp.int32, (keys, 1), 0) < scalars_ref[0]
    masks = lane_masks(q_ref.shape[1])
    turned = k_ref[...].T
    for start in range(0, queries, CHUNK):
        rows = pl.ds(start, CHUNK)
        parts = []
        for head, mask in enumerate(masks):
            query = keep(mask, q_ref[rows, :])
            d_mixed = keep(mask, dm_ref[rows, :])
            probs = softmax_turned(k_ref[...], query, valid)
            d_values = nn(probs.astype(BF16), d_mixed)
            d_probs = nt(v_ref[...], d_mixed)
            row_dot = jnp.sum(d_probs * probs, 0, keepdims=True)
            d_scores = (probs * (d_probs - row_dot)).astype(BF16)
            d_keys = nn(d_scores, query)
            parts.append(nn(turned[head * HD : (head + 1) * HD, :], d_scores))
            if start == 0 and head == 0:
                dk_sum[...] = d_keys
                dv_sum[...] = d_values
            else:
                dk_sum[...] += d_keys
                dv_sum[...] += d_values
        part = jnp.concatenate(parts, 0) * HD ** (-0.5)
        dq_turned[:, rows] = part.astype(BF16)
        dq_all[rows, :] = part.T.astype(BF16)
    d_queries = dq_all[...]
    d_keys = dk_sum[...].astype(BF16)
    d_values = dv_sum[...].astype(BF16)
    keys_turned, values_turned = d_keys.T, d_values.T
    sums_ref[0, 0:1] = jnp.sum(d_queries.astype(F32), 0, keepdims=True)
    sums_ref[0, 1:2] = jnp.sum(d_values.astype(F32), 0, keepdims=True)

    sub = HD // INNER
    heads = near_ref.shape[2] // (4 * sub)
    grads = [
        nn(dq_turned[...], own_ref[...]),
        nn(keys_turned, seq_ref[...]),
        nn(values_turned, seq_ref[...]),
        nn(mixed_ref[...], da_ref[...]),
    ]
    for which in range(2):
        head = 2 * step + which
        place = head // heads
        for kind, grad in enumerate(grads):
            rows = pl.ds(pl.multiple_of((kind * heads + head % heads) * sub, sub), sub)
            for block in range(INNER):
                target = near_ref if block < INNER // 2 else far_ref
                at = which * HD + block * sub
                target[block % (INNER // 2), place, rows, :] = grad[at : at + sub, :]

    own_part = tn(wq_ref[...], dq_turned[...])
    seq_part = tn(wk_ref[...], keys_turned) + tn(wv_ref[...], values_turned)

    @pl.when(step == 0)
    def _():
        own_part_ref[...] = own_part + (given[0][...] if last else given[0][...].T)
        seq_part_ref[...] = seq_part + given[1][...] if last else seq_part

    @pl.when(step > 0)
    def _():
        own_part_ref[...] += own_part
        seq_part_ref[...] += seq_part

    if last:

        @pl.when(step == pl.num_programs(0) - 1)
        def _():
            own = pl.ds(pl.multiple_of(scalars_ref[1], CHUNK), queries)
            seq_part_ref[:, own] += own_part_ref[...]


def attention_forward(me, lengths, queries, keys, values):
    count, width = queries.shape
    seq = count // lengths.shape[0]
    block = pl.BlockSpec((seq, width), lambda i: (i, 0))
    work = count * seq * width
    return pl.pallas_call(
        forward_kernel,
        grid=(lengths.shape[0],),
        in_specs=[pl.BlockSpec(memory_space=pltpu.SMEM)] * 2 + [block] * 3,
        out_specs=pl.BlockSpec((width, seq), lambda i: (0, i)),
        out_shape=jax.ShapeDtypeStruct((width, count), F32),
        compiler_params=pltpu.CompilerParams(vmem_limit_bytes=48 * 2**20),
        cost_estimate=pl.CostEstimate(flops=work, bytes_accessed=4 * 2**20, transcendentals=0),
    )(me, lengths, queries, keys, values)


def attention_backward(scalars, half, in_pairs, weights, whole, given):
    queries, keys, values, d_mixed, mixed = in_pairs
    count, width = queries.shape
    long = keys.shape[0]
    pairs = width // (4 * HD)
    begin = half * pairs
    places = 2
    rows = 4 * (width // 4) // INNER
    columns = lambda array: pl.BlockSpec((array.shape[0], 2 * HD), lambda j: (0, begin + j))
    of_rows = lambda array: pl.BlockSpec((2 * HD, array.shape[1]), lambda j: (begin + j, 0))
    full = lambda array: pl.BlockSpec(array.shape, lambda j: (0,) * len(array.shape))
    sent = jax.ShapeDtypeStruct((INNER // 2, places, rows, width), F32)
    parts = [jax.ShapeDtypeStruct((width, n), F32) for n in (count, long)]
    return pl.pallas_call(
        lambda *refs: backward_kernel(half == 1, *refs),
        grid=(pairs,),
        in_specs=[pl.BlockSpec(memory_space=pltpu.SMEM)]
        + [columns(array) for array in (queries, keys, values, d_mixed)]
        + [of_rows(array) for array in (mixed, *weights)]
        + [full(array) for array in (*whole, *given)],
        out_specs=[full(sent), full(sent), pl.BlockSpec((1, 2, 2 * HD), lambda j: (j, 0, 0))]
        + [full(part) for part in parts],
        out_shape=[sent, sent, jax.ShapeDtypeStruct((pairs, 2, 2 * HD), F32), *parts],
        scratch_shapes=[
            pltpu.VMEM((long, 2 * HD), F32),
            pltpu.VMEM((long, 2 * HD), F32),
            pltpu.VMEM((count, 2 * HD), BF16),
            pltpu.VMEM((2 * HD, count), BF16),
        ],
        compiler_params=pltpu.CompilerParams(vmem_limit_bytes=56 * 2**20),
        cost_estimate=pl.CostEstimate(flops=count * width, bytes_accessed=2**20, transcendentals=0),
    )(scalars, queries, keys, values, d_mixed, mixed, *weights, *whole, *given)


class ShareInputs:
    def __init__(self, part):
        quarters = part.reshape((4, part.shape[0] // 4, part.shape[1]))
        place = lax.axis_index("tensor")
        self.flipped = place >= 2
        end = jnp.where(self.flipped, 3, 0)
        near = lambda i: lax.dynamic_index_in_dim(quarters, jnp.abs(end - i), 0, keepdims=False)
        self.near = [near(i) for i in range(4)]
        self.outer = (place == 0) | (place == 3)
        swap = [(0, 1), (1, 0), (2, 3), (3, 2)]
        self.first = lax.ppermute(near(jnp.where(self.outer, 3, 0)), "tensor", swap)
        self.second = lax.ppermute(self.near[2], "tensor", [(0, 1), (3, 2)])

    def middle(self):
        across = [(1, 2), (2, 1)]
        self.far = lax.ppermute(self.near[3] + self.first, "tensor", across)
        self.third = lax.ppermute(self.near[1], "tensor", [(0, 1), (3, 2)])
        self.across = lax.ppermute(self.near[2] + self.second, "tensor", across)

    def result(self):
        last = lax.ppermute(self.far, "tensor", [(2, 3), (1, 0)])
        mine = jnp.where(self.outer, self.near[0] + self.first, self.near[1] + self.third)
        theirs = jnp.where(self.outer, last, self.across)
        return jnp.concatenate(
            [jnp.where(self.flipped, theirs, mine), jnp.where(self.flipped, mine, theirs)], 1
        )


def on_device(
    tokens,
    lengths,
    cotangent,
    qkv_weight,
    qv_bias,
    out_weight,
    out_bias,
    first_gain,
    first_shift,
    up_weight,
    up_bias,
    down_weight,
    down_bias,
    second_gain,
    second_shift,
):
    rows, width = tokens.shape
    seq = rows // lengths.shape[0]
    columns = qkv_weight.shape[2]
    heads = columns // HD
    units = up_weight.shape[1]
    share = rows // 4
    sub = HD // INNER
    count = units // INNER
    scale = jnp.asarray(HD ** (-0.5), BF16)
    place = lax.axis_index("tensor")
    me = lax.axis_index("dp") % INNER
    one = unit(lengths)

    few = heads * sub
    heads_of = lambda x: x.reshape(x.shape[:-2] + (heads, INNER, sub, width))
    out_heads = heads_of(out_weight)
    qkv_heads = heads_of(qkv_weight.transpose(0, 2, 1))
    qv_heads = qv_bias.reshape(2, heads, INNER, sub)
    up_turned = up_weight.T.reshape(INNER, count, width)
    down_blocks = down_weight.reshape(INNER, count, width)
    up_bias_blocks = up_bias.reshape(INNER, count)
    mine = lambda x, axis: lax.dynamic_index_in_dim(x, me, axis, keepdims=False)
    vectors = jnp.concatenate([mine(up_bias_blocks, 0), mine(qv_heads, 2).reshape(-1)])
    out_piece = jnp.concatenate(
        [
            mine(out_heads, 1).reshape(few, width).astype(F32) * one,
            jnp.pad(vectors[None], ((0, 7), (0, width - vectors.shape[0]))),
        ]
    )
    up_piece = mine(up_turned, 0).astype(F32) * one
    down_piece = mine(down_blocks, 0).astype(F32) * one
    qkv_piece = mine(qkv_heads, 2).reshape(3 * few, width).astype(F32) * one

    local_q = (nn(tokens, qkv_weight[0]) + qv_bias[0]).astype(BF16) * scale
    local_k = nn(tokens, qkv_weight[1]).astype(BF16)
    local_v = (nn(tokens, qkv_weight[2]) + qv_bias[1]).astype(BF16)

    out_places = gather_places(out_piece)
    up_places = gather_halves(after(up_piece, out_piece))
    down_places = gather_halves(after(down_piece, up_piece))
    out_first = gather_first(out_places, 0)
    local_mixed = attention_forward(me[None], lengths, local_q, local_k, local_v)

    def both_first(places, recv=lambda x: x):
        return [gather_first(held, route, recv) for route, held in enumerate(places)]

    def both_second(held, recv=lambda x: x):
        return [held[0], recv(flip(held[0], 2)), held[1], recv(flip(held[1], 1))]

    out_far = gather_second(out_first, 0)
    up_first = both_first(after(up_places, local_mixed))
    out_other = flip(after(out_far, up_first), 0)
    local_mixed = after(local_mixed, down_places) * one
    mixed_places = [lax.dynamic_slice_in_dim(local_mixed, place * share, share, 1)]
    for step in (1, 2, 3):
        theirs = lax.rem(place + 4 - step, 4)
        mixed_places.append(
            from_next(lax.dynamic_slice_in_dim(local_mixed, theirs * share, share, 1), step)
        )
    mixed_places = after(mixed_places, up_first, out_other)
    late = lambda x: after(x, mixed_places)
    up_far = both_second(up_first, late)
    down_first = both_first(after(down_places, up_first), late)
    up_other = [flip(part, 0) for part in up_far]
    down_far = both_second(down_first)
    qkv_places = gather_places(after(qkv_piece, mixed_places))

    def heads_together(near, pair, kinds):
        far = jnp.stack(pair).reshape(2, 2, 2, 3, kinds, heads, sub, width)
        far = (far.transpose(4, 3, 5, 0, 1, 2, 6, 7) * one).astype(BF16)
        far = far.reshape(kinds, 3 * columns, width)
        return jnp.concatenate([near.reshape(kinds, columns, width), far], 1)

    def heads_apart(array, places):
        trail = array.shape[1:]
        both = array.reshape((places, heads, 2, 2, 2, sub) + trail)
        both = both.transpose((2, 3, 4, 0, 1, 5) + tuple(range(6, 6 + len(trail))))
        return both.reshape((2, 2, 2, places, few) + trail)

    all_heads = jnp.concatenate([qkv_heads.reshape(3 * heads, INNER, sub, width), out_heads]).astype(F32)
    up_near, down_near, heads_near = relative_blocks(
        after(me[None], out_first), up_turned, down_blocks, all_heads
    )
    heads_near = heads_near.reshape(4, heads, INNER, sub, width).astype(BF16)
    qkv_near, out_near = heads_near[:3], heads_near[3]
    out_pair = (out_far, out_other)
    out_rows = heads_together(out_near[None], [far[:, :, :, :few] for far in out_pair], 1)[0]
    small_far = jnp.stack([far[:, :, :, few, : vectors.shape[0]] for far in out_pair])
    up_bias_near = relative(up_bias_blocks, 0).reshape(2, 2, 2, 1, count)
    up_bias_full = jnp.concatenate([up_bias_near, small_far[..., :count]], 3).reshape(2, 2 * units)
    qv_far = small_far[..., count:].reshape(2, 2, 2, 3, 2, heads, sub).transpose(4, 3, 5, 0, 1, 2, 6)
    qv_near = relative(qv_heads, 2)
    qv_full = jnp.concatenate([qv_near.reshape(2, columns), qv_far.reshape(2, 3 * columns)], 1)

    which = place // 2
    length = lax.dynamic_slice_in_dim(lengths, which, 1, 0)
    seq_tokens = lax.dynamic_slice_in_dim(tokens, which * seq, seq, 0)
    own_tokens = lax.dynamic_slice_in_dim(tokens, place * share, share, 0)
    own_cotangent = lax.dynamic_slice_in_dim(cotangent, place * share, share, 0)
    turned_mixed = (jnp.concatenate(mixed_places, 0) * one).astype(BF16)
    first = own_tokens.astype(F32) + (tn(turned_mixed, out_rows) + out_bias)
    normed, first_back = jax.vjp(layer_norm, first, first_gain, first_shift)
    normed_low = normed.astype(BF16)

    normed_low = after(normed_low, down_far)
    down_other = [flip(part, 0) for part in down_far]
    up_full = [units_together(up_near, 0, up_far), units_together(up_near, 1, up_other)]
    hidden, active, gelu_back = [], [], []
    for core in range(2):
        hidden.append(nt(normed_low, up_full[core]) + up_bias_full[core])
        value, back = jax.vjp(exact_gelu, hidden[core])
        active.append(value.astype(BF16))
        gelu_back.append(back)
        normed_low = after(normed_low, active[core], qkv_places)
    down_full = [units_together(down_near, 0, down_far)]
    qkv_first = gather_first(after(qkv_places, active[0]), 1)
    branch = nn(after(active[0], active[1], qkv_first), down_full[0])
    down_full.append(units_together(down_near, 1, after(down_other, branch)))
    branch = branch + nn(active[1], down_full[1])
    second = normed + (branch + down_bias)
    result, second_back = jax.vjp(layer_norm, second, second_gain, second_shift)
    output = (lax.all_gather(result, "tensor", axis=0, tiled=True) * one).astype(BF16)

    d_second, grad_second_gain, grad_second_shift = second_back(own_cotangent.astype(F32))
    d_branch = d_second.astype(BF16)
    grad_down_bias = jnp.sum(d_branch.astype(F32), 0)

    blocks = (2, 2, 4, count, width)
    down_sent = tn(active[1], d_branch).reshape(blocks)
    d_branch = after(d_branch, down_sent)
    d_hidden = [None, gelu_back[1](nt(d_branch, down_full[1]))[0].astype(BF16)]
    up_sent = tn(d_hidden[1], normed_low).reshape(blocks)
    qkv_far = gather_second(qkv_first, 1)
    d_branch = after(d_branch, up_sent, qkv_far)
    d_hidden[0] = gelu_back[0](nt(d_branch, down_full[0]))[0].astype(BF16)
    down_held = tn(active[0], after(d_branch, d_hidden[0])).reshape(blocks) + flip(down_sent, 0)
    up_held = tn(d_hidden[0], after(normed_low, down_held)).reshape(blocks) + flip(up_sent, 0)
    d_hidden = after(d_hidden, up_held)
    d_normed = nn(d_hidden[0], up_full[0]) + nn(d_hidden[1], up_full[1]) + d_second
    grad_up_bias = jnp.concatenate([jnp.sum(part.astype(F32), 0) for part in d_hidden])
    d_first, grad_first_gain, grad_first_shift = first_back(d_normed)
    d_attended = d_first.astype(BF16)
    grad_out_bias = jnp.sum(d_attended.astype(F32), 0)
    d_mixed = nt(d_attended, out_rows).astype(BF16)

    qkv_full = heads_together(qkv_near, (qkv_far, flip(qkv_far, 0)), 3)
    q_rows, k_rows, v_rows = qkv_full
    queries = (nt(own_tokens, q_rows) + qv_full[0]).astype(BF16) * scale
    keys = nt(seq_tokens, k_rows).astype(BF16)
    values = (nt(seq_tokens, v_rows) + qv_full[1]).astype(BF16)
    d_mixed = after(d_mixed, up_held, queries, keys, values)
    scalars = jnp.concatenate([length, ((place % 2) * share)[None]])
    attn_held, column_sums, given = [], [], (d_first,)
    for half in range(2):
        near, far, sums, *given = attention_backward(
            scalars,
            half,
            (queries, keys, values, d_mixed, turned_mixed),
            (q_rows, k_rows, v_rows),
            (own_tokens, seq_tokens, d_attended),
            given,
        )
        column_sums.append(sums)
        d_mixed = after(d_mixed, far)
        blocks = (2, 2) + near.shape[1:]
        attn_held.append(near.reshape(blocks) + flip(far, 0).reshape(blocks))
    input_part = given[1]
    late = lambda x: after(x, input_part, attn_held[0])
    down_held = scatter_first(down_held, 0, late)
    up_held = scatter_first(up_held, 1, late)

    attn_held[0] = scatter_first(attn_held[0], 0)
    attn_held[1] = scatter_first(attn_held[1], 1)
    share_inputs = ShareInputs(input_part)
    late = lambda x: after(x, share_inputs.first)
    down_held = scatter_second(down_held, 0, late)
    up_held = scatter_second(up_held, 1, late)
    mlp_places = jnp.concatenate([up_held, down_held], 1)
    share_inputs.middle()
    attn_held = [scatter_second(held, half) for half, held in enumerate(attn_held)]
    attn_places = [held[i] for held in attn_held for i in range(2)]
    late = lambda x: after(x, attn_places, share_inputs.third, share_inputs.across)
    mlp_sums = scatter_places(mlp_places, late)
    mlp_all = gather_in_order(mlp_sums, (1, 2))
    attn_sums = scatter_places(attn_places, lambda x: after(x, mlp_sums))
    attn_all = gather_in_order(after(attn_sums, output), (2, 1))
    grad_tokens = share_inputs.result().T
    attn_all = attn_all.reshape(INNER, 4, heads, sub, width).transpose(1, 2, 0, 3, 4)
    attn_all = attn_all.reshape(4, columns, width)

    qv_sums = jnp.concatenate(column_sums).transpose(0, 2, 1).reshape(width, 2)
    qv_sums = heads_apart(qv_sums, 4).transpose(0, 1, 2, 3, 5, 4).reshape(4 * INNER, 2 * few)
    vector_blocks = jnp.concatenate([grad_up_bias.reshape(4 * INNER, count), qv_sums], 1)
    index = jnp.arange(4 * INNER, dtype=jnp.int32)
    apart = (index % INNER) ^ me
    step = (index // INNER + 4 - place) % 4
    order = (apart & 1) * 16 + (apart >> 2) * 8 + ((apart >> 1) & 1) * 4 + step
    vector_blocks = jnp.take(vector_blocks, order, axis=0)
    vectors = [
        grad_out_bias,
        grad_first_gain,
        grad_first_shift,
        grad_down_bias,
        grad_second_gain,
        grad_second_shift,
    ]
    small = sum_everywhere(
        jnp.concatenate([vector_blocks.reshape(-1), *vectors]).reshape(-1, 128),
        (mlp_places, attn_places, mlp_sums, attn_sums),
    ).reshape(-1)
    blocks = small[: vector_blocks.size].reshape(4, INNER, -1)
    blocks = lax.dynamic_index_in_dim(blocks, place, 0, keepdims=False)
    qv_all = blocks[:, count:].reshape(INNER, 2, heads, sub)
    small = small[small.size - 6 * width :].reshape(6, width)
    return (
        output,
        grad_tokens,
        attn_all[:3].transpose(0, 2, 1),
        qv_all.transpose(1, 2, 0, 3).reshape(2, columns),
        attn_all[3],
        small[0],
        small[1],
        small[2],
        mlp_all[:, :count].reshape(units, width).T,
        blocks[:, :count].reshape(-1),
        mlp_all[:, count:].reshape(units, width),
        small[3],
        small[4],
        small[5],
    )


def solution(mesh):
    placed = (
        P("dp", None),
        P("dp"),
        P("dp", None),
        P(None, None, "tensor"),
        P(None, "tensor"),
        P("tensor", None),
        P(),
        P(),
        P(),
        P(None, "tensor"),
        P("tensor"),
        P("tensor", None),
        P(),
        P(),
        P(),
    )
    return jax.shard_map(
        on_device,
        mesh=mesh,
        in_specs=placed,
        out_specs=(
            P("dp", None),
            P("dp", "tensor"),
            P(None, None, "tensor"),
            P(None, "tensor"),
            P("tensor", None),
            P(),
            P(),
            P(),
            P(None, "tensor"),
            P("tensor"),
            P("tensor", None),
            P(),
            P(),
            P(),
        ),
        check_vma=False,
    )
```

```python
import jax
import jax.numpy as jnp
from jax import lax
from jax.experimental import pallas as pl
from jax.experimental.pallas import tpu as pltpu
from jax.sharding import PartitionSpec as P

HD = 64
EPS = 1e-05
MASKED = -1000000000.0
BITS = 3
INNER = 1 << BITS
F32 = jnp.float32
BF16 = jnp.bfloat16


def layer_norm(hidden, gain, shift):
    center = hidden - jnp.mean(hidden, -1, keepdims=True)
    spread = jnp.mean(center * center, -1, keepdims=True)
    return center * lax.rsqrt(spread + EPS) * gain + shift


def exact_gelu(inputs):
    return jax.nn.gelu(inputs, approximate=False)


def nn(left, right):
    return lax.dot_general(left, right, (((1,), (0,)), ((), ())), preferred_element_type=F32)


def nt(left, right):
    return lax.dot_general(left, right, (((1,), (1,)), ((), ())), preferred_element_type=F32)


def tn(left, right):
    return lax.dot_general(left, right, (((0,), (0,)), ((), ())), preferred_element_type=F32)


APART = [c | (x << 1) | (y << 2) for c in (0, 1) for y in (0, 1) for x in (0, 1)]


def unit(lengths):
    return jnp.where(lengths[0] > 0, 1.0, 0.0).astype(F32)


def after(x, *others):
    return lax.optimization_barrier((x, others))[0]


def flip(x, bit):
    size = lax.axis_size("dp")
    return lax.ppermute(x, "dp", [(i, i ^ (1 << bit)) for i in range(size)])


def from_next(x, step):
    size = lax.axis_size("tensor")
    return lax.ppermute(x, "tensor", [((i + step) % size, i) for i in range(size)])


def to_next(x, step):
    size = lax.axis_size("tensor")
    return lax.ppermute(x, "tensor", [(i, (i + step) % size) for i in range(size)])


def relative(x, axis):
    me = lax.axis_index("dp") % INNER
    return jnp.concatenate([lax.dynamic_slice_in_dim(x, me ^ apart, 1, axis) for apart in APART], axis)


def owner(core, step, me_ref):
    return me_ref[0] ^ (core | ((step % 2) << 1) | ((step // 2) << 2))


def heads_kernel(me_ref, near_a_ref, near_b_ref, *refs):
    parts, out_ref = (refs[:4], refs[4:8]), refs[8]
    kinds, places, heads = out_ref.shape[:3]
    sub = near_a_ref.shape[2]

    def block(near_ref, held, kind, at, head):
        if at == 0:
            return near_ref[kind * heads + head, 0]
        rows = pl.ds((kind % 2 * heads + head) * sub, sub)
        return held[kind // 2][0, at - 1, rows, :]

    for step in range(4):

        @pl.when(pl.program_id(0) == step)
        def _():
            own, other = [(held[step // 2], held[2 + step % 2]) for held in parts]
            for kind in range(kinds):
                for at in range(places):
                    for head in range(heads):
                        pair = [
                            block(near_a_ref, own, kind, at, head),
                            block(near_b_ref, other, kind, at, head),
                        ]
                        out_ref[kind, at, head, 0] = jnp.concatenate(pair, 0).astype(BF16)


def part_specs(parts):
    by_x = pl.BlockSpec((1,) + parts[0].shape[1:], lambda k, me_ref: (k % 2, 0, 0, 0))
    by_y = pl.BlockSpec((1,) + parts[2].shape[1:], lambda k, me_ref: (k // 2, 0, 0, 0))
    return [by_x, by_x, by_y, by_y]


def heads_together(me, near, own, other):
    count, _, sub, width = near.shape
    heads = count // 4
    near_spec = lambda core: pl.BlockSpec(
        (count, 1, sub, width), lambda k, me_ref: (0, owner(core, k, me_ref), 0, 0)
    )
    full = pl.pallas_call(
        heads_kernel,
        grid_spec=pltpu.PrefetchScalarGridSpec(
            num_scalar_prefetch=1,
            grid=(4,),
            in_specs=[near_spec(0), near_spec(1)] + part_specs(own) + part_specs(other),
            out_specs=pl.BlockSpec((4, 4, heads, 1, 2 * sub, width), lambda k, me_ref: (0, 0, 0, k, 0, 0)),
        ),
        out_shape=jax.ShapeDtypeStruct((4, 4, heads, 4, 2 * sub, width), BF16),
        compiler_params=pltpu.CompilerParams(vmem_limit_bytes=48 * 2**20),
    )(me, near, near, *own, *other)
    return full.reshape(4, 4 * heads * INNER * sub, width)


def units_kernel(me_ref, near_ref, a_ref, a_far_ref, b_ref, b_far_ref, out_ref):
    step = pl.program_id(0)
    half = a_ref.shape[2]
    out_ref[0, 0] = near_ref[0]

    @pl.when(step < 2)
    def _():
        out_ref[0, 1:, :half] = a_ref[0].astype(BF16)

    @pl.when(step >= 2)
    def _():
        out_ref[0, 1:, :half] = a_far_ref[0].astype(BF16)

    @pl.when(step % 2 == 0)
    def _():
        out_ref[0, 1:, half:] = b_ref[0].astype(BF16)

    @pl.when(step % 2 == 1)
    def _():
        out_ref[0, 1:, half:] = b_far_ref[0].astype(BF16)


def units_together(me, near, core, parts):
    count, width = near.shape[1:]
    full = pl.pallas_call(
        units_kernel,
        grid_spec=pltpu.PrefetchScalarGridSpec(
            num_scalar_prefetch=1,
            grid=(4,),
            in_specs=[pl.BlockSpec((1, count, width), lambda k, me_ref: (owner(core, k, me_ref), 0, 0))]
            + part_specs(parts),
            out_specs=pl.BlockSpec((1, 4, count, width), lambda k, me_ref: (k, 0, 0, 0)),
        ),
        out_shape=jax.ShapeDtypeStruct((4, 4, count, width), BF16),
        compiler_params=pltpu.CompilerParams(vmem_limit_bytes=48 * 2**20),
    )(me, near, *parts)
    return full.reshape(16 * count, width)


def gather_halves(piece, half):
    places = [from_next(piece, step) for step in (1, 2, 3)]
    return [jnp.stack([place[:half] for place in places]), jnp.stack([place[half:] for place in places])]


def both_first(places, recv=lambda x: x):
    return [jnp.stack([held, recv(flip(held, bit))]) for held, bit in zip(places, (1, 2))]


def both_second(held, recv=lambda x: x):
    return [held[0], recv(flip(held[0], 2)), held[1], recv(flip(held[1], 1))]


def scatter_first(held, route, recv=lambda x: x):
    if route:
        got = recv(flip(held[:, 1], 1))
        return held[0, 0] + got[0], held[1, 0] + got[1]
    got = recv(flip(held[1], 2))
    return held[0, 0] + got[0], held[0, 1] + got[1]


def scatter_second(parts, route, recv=lambda x: x):
    return parts[0] + recv(flip(parts[1], 2 if route else 1))


def scatter_place(total, places, step, recv=lambda x: x):
    return places[step] + recv(to_next(total, 1))


def scatter_outer(total):
    bit = BITS
    while (1 << bit) < lax.axis_size("dp"):
        total = total + flip(total, bit)
        bit += 1
    return total


def gather_in_order(piece, order, others=()):
    held = piece[None]
    for bit in (*order, 0):
        if bit == 0 and others:
            held = after(held, others)
        held = jnp.concatenate([held, flip(held, bit)], 0)
    me = lax.axis_index("dp") % INNER
    blocks = []
    for index in range(INNER):
        apart = me ^ index
        place = sum(((apart >> bit) & 1) << at for at, bit in enumerate((*order, 0)))
        blocks.append(lax.dynamic_index_in_dim(held, place, 0))
    return jnp.concatenate(blocks, 0)


def sum_everywhere(x, others):
    others = list(others)
    for axis in ("dp", "tensor"):
        size = lax.axis_size(axis)
        step = 1
        while step < size:
            got = lax.ppermute(x, axis, [(i, i ^ step) for i in range(size)])
            x = x + (after(got, others.pop(0)) if others else got)
            step *= 2
    return x


CHUNK = 256


def lane_masks(width):
    lane = lax.broadcasted_iota(jnp.int32, (1, width), 1)
    return [(lane >= start) & (lane < start + HD) for start in range(0, width, HD)]


def keep(mask, x):
    return jnp.where(mask, x, jnp.zeros_like(x))


def softmax_turned(keys, query, valid):
    scores = jnp.where(valid, nt(keys, query), MASKED)
    expo = jnp.exp(scores - jnp.max(scores, 0, keepdims=True))
    return expo * (1.0 / jnp.sum(expo, 0, keepdims=True))


def forward_kernel(length_ref, q_ref, k_ref, v_ref, mixed_ref):
    keys = k_ref.shape[0]
    valid = lax.broadcasted_iota(jnp.int32, (keys, 1), 0) < length_ref[0]
    masks = lane_masks(q_ref.shape[1])
    turned = v_ref[...].T
    for start in range(0, q_ref.shape[0], CHUNK):
        rows = pl.ds(start, CHUNK)
        for head, mask in enumerate(masks):
            probs = softmax_turned(k_ref[...], keep(mask, q_ref[rows, :]), valid).astype(BF16)
            own = slice(head * HD, (head + 1) * HD)
            mixed_ref[own, rows] = nn(turned[own, :], probs).astype(BF16)


def backward_kernel(
    scalars_ref,
    q_ref,
    k_ref,
    v_ref,
    dm_ref,
    mixed_ref,
    wq_ref,
    wk_ref,
    wv_ref,
    own_ref,
    seq_ref,
    da_ref,
    first_ref,
    near_ref,
    far_ref,
    sums_ref,
    seq_part_ref,
    own_part_ref,
    dk_sum,
    dv_sum,
    dq_all,
    dq_turned,
):
    keys = k_ref.shape[0]
    queries = q_ref.shape[0]
    step = pl.program_id(0)
    valid = lax.broadcasted_iota(jnp.int32, (keys, 1), 0) < scalars_ref[0]
    masks = lane_masks(q_ref.shape[1])
    turned = k_ref[...].T
    for start in range(0, queries, CHUNK):
        rows = pl.ds(start, CHUNK)
        parts = []
        for head, mask in enumerate(masks):
            query = keep(mask, q_ref[rows, :])
            d_mixed = keep(mask, dm_ref[rows, :])
            probs = softmax_turned(k_ref[...], query, valid)
            d_values = nn(probs.astype(BF16), d_mixed)
            d_probs = nt(v_ref[...], d_mixed)
            row_dot = jnp.sum(d_probs * probs, 0, keepdims=True)
            d_scores = (probs * (d_probs - row_dot)).astype(BF16)
            d_keys = nn(d_scores, query)
            parts.append(nn(turned[head * HD : (head + 1) * HD, :], d_scores))
            if start == 0 and head == 0:
                dk_sum[...] = d_keys
                dv_sum[...] = d_values
            else:
                dk_sum[...] += d_keys
                dv_sum[...] += d_values
        part = jnp.concatenate(parts, 0) * HD ** (-0.5)
        dq_turned[:, rows] = part.astype(BF16)
        dq_all[rows, :] = part.T.astype(BF16)
    d_queries = dq_all[...]
    d_keys = dk_sum[...].astype(BF16)
    d_values = dv_sum[...].astype(BF16)
    keys_turned, values_turned = d_keys.T, d_values.T
    sums_ref[0, 0:1] = jnp.sum(d_queries.astype(F32), 0, keepdims=True)
    sums_ref[0, 1:2] = jnp.sum(d_values.astype(F32), 0, keepdims=True)

    sub = HD // INNER
    heads = near_ref.shape[2] // (4 * sub)
    grads = [
        nn(dq_turned[...], own_ref[...]),
        nn(keys_turned, seq_ref[...]),
        nn(values_turned, seq_ref[...]),
        nn(mixed_ref[...], da_ref[...]),
    ]
    for which in range(2):
        head = 2 * step + which
        place = head // heads
        for kind, grad in enumerate(grads):
            rows = pl.ds(pl.multiple_of((kind * heads + head % heads) * sub, sub), sub)
            for block in range(INNER):
                target = far_ref if block % 2 else near_ref
                at = which * HD + block * sub
                target[block // 2, place, rows, :] = grad[at : at + sub, :]

    own_part = tn(wq_ref[...], dq_turned[...])
    seq_part = tn(wk_ref[...], keys_turned) + tn(wv_ref[...], values_turned)

    @pl.when(step == 0)
    def _():
        own_part_ref[...] = own_part + first_ref[...].T
        seq_part_ref[...] = seq_part

    @pl.when(step > 0)
    def _():
        own_part_ref[...] += own_part
        seq_part_ref[...] += seq_part

    @pl.when(step == pl.num_programs(0) - 1)
    def _():
        own = pl.ds(pl.multiple_of(scalars_ref[1], CHUNK), queries)
        seq_part_ref[:, own] += own_part_ref[...]


def attention_forward(length, queries, keys, values):
    count, width = queries.shape
    columns = lambda array: pl.BlockSpec((array.shape[0], 2 * HD), lambda j: (0, j))
    return pl.pallas_call(
        forward_kernel,
        grid=(width // (2 * HD),),
        in_specs=[pl.BlockSpec(memory_space=pltpu.SMEM)]
        + [columns(array) for array in (queries, keys, values)],
        out_specs=pl.BlockSpec((2 * HD, count), lambda j: (j, 0)),
        out_shape=jax.ShapeDtypeStruct((width, count), BF16),
        compiler_params=pltpu.CompilerParams(vmem_limit_bytes=48 * 2**20),
        cost_estimate=pl.CostEstimate(flops=count * width, bytes_accessed=2**20, transcendentals=0),
    )(length, queries, keys, values)


def attention_backward(scalars, in_pairs, weights, whole):
    queries, keys, values, d_mixed, mixed = in_pairs
    count, width = queries.shape
    long = keys.shape[0]
    pairs = width // (2 * HD)
    columns = lambda array: pl.BlockSpec((array.shape[0], 2 * HD), lambda j: (0, j))
    of_rows = lambda array: pl.BlockSpec((2 * HD, array.shape[1]), lambda j: (j, 0))
    full = lambda array: pl.BlockSpec(array.shape, lambda j: (0,) * len(array.shape))
    sent = jax.ShapeDtypeStruct((INNER // 2, 4, width // INNER, width), F32)
    part = jax.ShapeDtypeStruct((width, long), F32)
    return pl.pallas_call(
        backward_kernel,
        grid=(pairs,),
        in_specs=[pl.BlockSpec(memory_space=pltpu.SMEM)]
        + [columns(array) for array in (queries, keys, values, d_mixed)]
        + [of_rows(array) for array in (mixed, *weights)]
        + [full(array) for array in whole],
        out_specs=[full(sent), full(sent), pl.BlockSpec((1, 2, 2 * HD), lambda j: (j, 0, 0)), full(part)],
        out_shape=[sent, sent, jax.ShapeDtypeStruct((pairs, 2, 2 * HD), F32), part],
        scratch_shapes=[
            pltpu.VMEM((width, count), F32),
            pltpu.VMEM((long, 2 * HD), F32),
            pltpu.VMEM((long, 2 * HD), F32),
            pltpu.VMEM((count, 2 * HD), BF16),
            pltpu.VMEM((2 * HD, count), BF16),
        ],
        compiler_params=pltpu.CompilerParams(vmem_limit_bytes=56 * 2**20),
        cost_estimate=pl.CostEstimate(flops=count * width, bytes_accessed=2**20, transcendentals=0),
    )(scalars, queries, keys, values, d_mixed, mixed, *weights, *whole)


class ShareInputs:
    def __init__(self, part):
        quarters = part.reshape((4, part.shape[0] // 4, part.shape[1]))
        place = lax.axis_index("tensor")
        self.flipped = place >= 2
        end = jnp.where(self.flipped, 3, 0)
        near = lambda i: lax.dynamic_index_in_dim(quarters, jnp.abs(end - i), 0, keepdims=False)
        self.near = [near(i) for i in range(4)]
        self.outer = (place == 0) | (place == 3)
        swap = [(0, 1), (1, 0), (2, 3), (3, 2)]
        self.first = lax.ppermute(near(jnp.where(self.outer, 3, 0)), "tensor", swap)
        self.second = lax.ppermute(self.near[2], "tensor", [(0, 1), (3, 2)])

    def second_there(self, first):
        self.far_sum = self.near[3] + first
        self.far = lax.ppermute(self.far_sum, "tensor", [(1, 2), (2, 1)])
        self.third = lax.ppermute(self.near[1], "tensor", [(0, 1), (3, 2)])

    def middle(self):
        self.across = lax.ppermute(self.near[2] + self.second, "tensor", [(1, 2), (2, 1)])

    def result(self):
        last = lax.ppermute(self.far, "tensor", [(2, 3), (1, 0)])
        mine = jnp.where(self.outer, self.near[0] + self.first, self.near[1] + self.third)
        theirs = jnp.where(self.outer, last, self.across)
        return jnp.concatenate(
            [jnp.where(self.flipped, theirs, mine), jnp.where(self.flipped, mine, theirs)], 1
        )


def on_device(
    tokens,
    lengths,
    cotangent,
    qkv_weight,
    qv_bias,
    out_weight,
    out_bias,
    first_gain,
    first_shift,
    up_weight,
    up_bias,
    down_weight,
    down_bias,
    second_gain,
    second_shift,
):
    rows, width = tokens.shape
    seq = rows // lengths.shape[0]
    columns = qkv_weight.shape[2]
    heads = columns // HD
    units = up_weight.shape[1]
    share = rows // 4
    sub = HD // INNER
    count = units // INNER
    scale = jnp.asarray(HD ** (-0.5), BF16)
    place = lax.axis_index("tensor")
    me = lax.axis_index("dp") % INNER
    one = unit(lengths)

    few = heads * sub
    all_heads = jnp.concatenate([qkv_weight.transpose(0, 2, 1), out_weight[None]]).astype(F32) * one
    all_heads = all_heads.reshape(4 * heads, INNER, sub, width)
    qv_heads = qv_bias.reshape(2, heads, INNER, sub)
    up_turned = up_weight.T.reshape(INNER, count, width)
    down_blocks = down_weight.reshape(INNER, count, width)
    up_bias_blocks = up_bias.reshape(INNER, count)
    mine = lambda x, axis: lax.dynamic_index_in_dim(x, me, axis, keepdims=False)
    vectors = jnp.concatenate([mine(up_bias_blocks, 0), mine(qv_heads, 2).reshape(-1)])
    heads_piece = mine(all_heads, 1).reshape(4 * few, width)
    vector_rows = jnp.pad(vectors[None], ((0, 7), (0, width - vectors.shape[0])))
    heads_piece = jnp.concatenate([heads_piece[: 2 * few], vector_rows, heads_piece[2 * few :]])
    up_piece = mine(up_turned, 0).astype(F32) * one
    down_piece = mine(down_blocks, 0).astype(F32) * one

    heads_places = gather_halves(heads_piece, 2 * few + 8)
    heads_first = both_first(heads_places)
    up_places = gather_halves(after(up_piece, heads_places), count // 2)
    heads_far = both_second(heads_first)
    heads_other = [flip(part, 0) for part in heads_far]

    spot = (slice(None), slice(None), 2 * few, slice(vectors.shape[0]))
    small_far = jnp.stack([jnp.stack([part[spot] for part in far[:2]]) for far in (heads_far, heads_other)])
    up_bias_near = relative(up_bias_blocks, 0).reshape(2, 2, 2, 1, count)
    up_bias_full = jnp.concatenate([up_bias_near, small_far[..., :count]], 3).reshape(2, 2 * units)
    qv_far = small_far[..., count:].reshape(2, 2, 2, 3, 2, heads, sub)
    qv_near = relative(qv_heads, 2).reshape(2, heads, 2, 2, 2, sub).transpose(0, 1, 3, 4, 2, 5)
    qv_full = [qv_near.reshape(2, columns), qv_far.transpose(4, 3, 5, 1, 2, 0, 6).reshape(2, 3 * columns)]
    qv_full = jnp.concatenate(qv_full, 1)

    def heads_apart(array, places):
        trail = array.shape[1:]
        both = array.reshape((places, heads, 2, 2, 2, sub) + trail)
        both = both.transpose((4, 2, 3, 0, 1, 5) + tuple(range(6, 6 + len(trail))))
        return both.reshape((2, 2, 2, places, few) + trail)

    which = place // 2
    length = lax.dynamic_slice_in_dim(lengths, which, 1, 0)
    seq_tokens = lax.dynamic_slice_in_dim(tokens, which * seq, seq, 0)
    own_tokens = lax.dynamic_slice_in_dim(tokens, place * share, share, 0)
    own_cotangent = lax.dynamic_slice_in_dim(cotangent, place * share, share, 0)
    whole_heads = heads_together(me[None], all_heads, heads_far, heads_other)
    down_places = gather_halves(after(down_piece, up_places, whole_heads), count // 2)
    up_first = both_first(after(up_places, heads_far), lambda x: after(x, whole_heads))
    q_rows, k_rows, v_rows, out_rows = after(whole_heads, up_first)
    queries = (nt(own_tokens, q_rows) + qv_full[0]).astype(BF16) * scale
    keys = nt(seq_tokens, k_rows).astype(BF16)
    values = (nt(seq_tokens, v_rows) + qv_full[1]).astype(BF16)
    turned_mixed = attention_forward(length, after(queries, down_places, keys, values), keys, values)
    late = lambda x: after(x, turned_mixed)
    up_far = both_second(up_first, late)
    down_first = both_first(after(down_places, up_first), late)
    turned_mixed = after(turned_mixed, up_far, down_first)
    up_other = [flip(part, 0) for part in up_far]
    first = own_tokens.astype(F32) + (tn(turned_mixed, out_rows) + out_bias)
    normed, first_back = jax.vjp(layer_norm, first, first_gain, first_shift)
    normed_low = normed.astype(BF16)

    up_full = [units_together(me[None], up_turned, core, parts) for core, parts in enumerate((up_far, up_other))]
    hidden, active, gelu_back = [], [], []
    down_far = None
    for core in range(2):
        hidden.append(nt(normed_low, up_full[core]) + up_bias_full[core])
        value, back = jax.vjp(exact_gelu, hidden[core])
        active.append(value.astype(BF16))
        gelu_back.append(back)
        if core == 0:
            down_far = both_second(down_first, lambda x: after(x, active[0]))
        normed_low = after(normed_low, active[core], down_far)
    down_other = [flip(part, 0) for part in down_far]
    down_full = [units_together(me[None], down_blocks, 0, down_far)]
    branch = nn(after(active[0], active[1]), down_full[0])
    down_full.append(units_together(me[None], down_blocks, 1, after(down_other, branch)))
    branch = branch + nn(active[1], down_full[1])
    second = normed + (branch + down_bias)
    result, second_back = jax.vjp(layer_norm, second, second_gain, second_shift)
    gathered = lax.all_gather(result, "tensor", axis=0, tiled=True)

    d_second, grad_second_gain, grad_second_shift = second_back(own_cotangent.astype(F32))
    d_branch = d_second.astype(BF16)
    grad_down_bias = jnp.sum(d_branch.astype(F32), 0)

    blocks = (2, 2, 4, count, width)
    down_sent = tn(active[1], d_branch)
    d_branch = after(d_branch, down_sent)
    d_hidden = [None, gelu_back[1](nt(d_branch, down_full[1]))[0].astype(BF16)]
    up_sent = tn(d_hidden[1], normed_low)
    d_branch = after(d_branch, up_sent)
    d_hidden[0] = gelu_back[0](nt(d_branch, down_full[0]))[0].astype(BF16)
    down_held = (tn(active[0], after(d_branch, d_hidden[0])) + flip(down_sent, 0)).reshape(blocks)
    up_held = (tn(d_hidden[0], after(normed_low, down_held)) + flip(up_sent, 0)).reshape(blocks)
    d_hidden = after(d_hidden, up_held)
    d_normed = nn(d_hidden[0], up_full[0]) + nn(d_hidden[1], up_full[1]) + d_second
    grad_up_bias = jnp.concatenate([jnp.sum(part.astype(F32), 0) for part in d_hidden])
    d_first, grad_first_gain, grad_first_shift = first_back(d_normed)
    d_attended = d_first.astype(BF16)
    grad_out_bias = jnp.sum(d_attended.astype(F32), 0)
    d_mixed = nt(d_attended, out_rows).astype(BF16)

    d_mixed = after(d_mixed, up_held)
    scalars = jnp.concatenate([length, ((place % 2) * share)[None]])
    near, far, column_sums, input_part = attention_backward(
        scalars,
        (queries, keys, values, d_mixed, turned_mixed),
        (q_rows, k_rows, v_rows),
        (own_tokens, seq_tokens, d_attended, d_first),
    )

    late = lambda x: after(x, input_part)
    down_held = scatter_first(down_held, 0, late)
    up_held = scatter_first(up_held, 1, late)
    near, far, column_sums, input_part = after(
        (near, far, column_sums, input_part), down_held, up_held, gathered
    )
    output = (gathered * one).astype(BF16)
    got = flip(far, 0)
    cut = lambda array, half: array[:, 2 * half : 2 * half + 2].reshape((2, 2, 2) + array.shape[2:])
    attn_held = [cut(near, half) + cut(got, half) for half in range(2)]
    attn_sent = attn_held
    share_inputs = ShareInputs(input_part)
    late = lambda x: after(x, attn_held)
    down_held = scatter_second(down_held, 0, late)
    up_held = scatter_second(up_held, 1, late)
    mlp_places = jnp.concatenate([up_held, down_held], 1)
    share_inputs.second_there(after(share_inputs.first, mlp_places))
    mlp_sums = scatter_place(mlp_places[3], mlp_places, 2)
    late = lambda x: after(x, share_inputs.far_sum)
    attn_held = [scatter_first(held, half, late) for half, held in enumerate(attn_held)]
    mlp_sums = scatter_place(after(mlp_sums, attn_held), mlp_places, 1)
    late = lambda x: after(x, mlp_sums)
    attn_held = [scatter_second(held, half, late) for half, held in enumerate(attn_held)]
    qv_sums = column_sums.transpose(0, 2, 1).reshape(width, 2)
    qv_sums = heads_apart(qv_sums, 4).transpose(0, 1, 2, 3, 5, 4).reshape(4 * INNER, 2 * few)
    vector_blocks = jnp.concatenate([grad_up_bias.reshape(4 * INNER, count), qv_sums], 1)
    index = jnp.arange(4 * INNER, dtype=jnp.int32)
    apart = (index % INNER) ^ me
    step = (index // INNER + 4 - place) % 4
    order = (apart & 1) * 16 + (apart >> 2) * 8 + ((apart >> 1) & 1) * 4 + step
    vector_blocks = jnp.take(vector_blocks, order, axis=0)
    vectors = [
        grad_out_bias,
        grad_first_gain,
        grad_first_shift,
        grad_down_bias,
        grad_second_gain,
        grad_second_shift,
    ]
    small_sum = sum_everywhere(
        jnp.concatenate([vector_blocks.reshape(-1), *vectors]).reshape(-1, 128),
        (attn_sent, mlp_places, mlp_sums),
    )
    small = small_sum.reshape(-1)
    attn_held = after(attn_held, small_sum)
    attn_places = [held[i] for held in attn_held for i in range(2)]
    share_inputs.middle()
    mlp_sums = scatter_place(mlp_sums, mlp_places, 0, lambda x: after(x, attn_places))
    mlp_sums = scatter_outer(mlp_sums)
    attn_sums = attn_places[3]
    for step in (2, 1, 0):
        attn_sums = scatter_place(attn_sums, attn_places, step)
    attn_sums = scatter_outer(attn_sums)
    mlp_all = gather_in_order(mlp_sums, (1, 2))
    grad_up = mlp_all[:, :count].reshape(units, width).T
    grad_down = mlp_all[:, count:].reshape(units, width)
    attn_all = gather_in_order(after(attn_sums, output), (2, 1), (grad_up, grad_down))
    grad_tokens = share_inputs.result().T
    attn_all = attn_all.reshape(INNER, 4, heads, sub, width).transpose(1, 2, 0, 3, 4)
    attn_all = attn_all.reshape(4, columns, width)

    blocks = small[: vector_blocks.size].reshape(4, INNER, -1)
    blocks = lax.dynamic_index_in_dim(blocks, place, 0, keepdims=False)
    qv_all = blocks[:, count:].reshape(INNER, 2, heads, sub)
    small = small[small.size - 6 * width :].reshape(6, width)
    return (
        output,
        grad_tokens,
        attn_all[:3].transpose(0, 2, 1),
        qv_all.transpose(1, 2, 0, 3).reshape(2, columns),
        attn_all[3],
        small[0],
        small[1],
        small[2],
        grad_up,
        blocks[:, :count].reshape(-1),
        grad_down,
        small[3],
        small[4],
        small[5],
    )


def solution(mesh):
    placed = (
        P("dp", None),
        P("dp"),
        P("dp", None),
        P(None, None, "tensor"),
        P(None, "tensor"),
        P("tensor", None),
        P(),
        P(),
        P(),
        P(None, "tensor"),
        P("tensor"),
        P("tensor", None),
        P(),
        P(),
        P(),
    )
    return jax.shard_map(
        on_device,
        mesh=mesh,
        in_specs=placed,
        out_specs=(
            P("dp", None),
            P("dp", "tensor"),
            P(None, None, "tensor"),
            P(None, "tensor"),
            P("tensor", None),
            P(),
            P(),
            P(),
            P(None, "tensor"),
            P("tensor"),
            P("tensor", None),
            P(),
            P(),
            P(),
        ),
        check_vma=False,
    )
```

```python
import jax
import jax.numpy as jnp
from jax import lax
from jax.experimental import pallas as pl
from jax.experimental.pallas import tpu as pltpu
from jax.sharding import PartitionSpec as P

HD = 64
EPS = 1e-05
MASKED = -1000000000.0
BITS = 3
INNER = 1 << BITS
F32 = jnp.float32
BF16 = jnp.bfloat16


def layer_norm(hidden, gain, shift):
    center = hidden - jnp.mean(hidden, -1, keepdims=True)
    spread = jnp.mean(center * center, -1, keepdims=True)
    return center * lax.rsqrt(spread + EPS) * gain + shift


def exact_gelu(inputs):
    return jax.nn.gelu(inputs, approximate=False)


def nn(left, right):
    return lax.dot_general(left, right, (((1,), (0,)), ((), ())), preferred_element_type=F32)


def nt(left, right):
    return lax.dot_general(left, right, (((1,), (1,)), ((), ())), preferred_element_type=F32)


def tn(left, right):
    return lax.dot_general(left, right, (((0,), (0,)), ((), ())), preferred_element_type=F32)


APART = [c | (x << 1) | (y << 2) for c in (0, 1) for y in (0, 1) for x in (0, 1)]


def unit(lengths):
    return jnp.where(lengths[0] > 0, 1.0, 0.0).astype(F32)


def after(x, *others):
    return lax.optimization_barrier((x, others))[0]


def flip(x, bit):
    size = lax.axis_size("dp")
    return lax.ppermute(x, "dp", [(i, i ^ (1 << bit)) for i in range(size)])


def from_next(x, step):
    size = lax.axis_size("tensor")
    return lax.ppermute(x, "tensor", [((i + step) % size, i) for i in range(size)])


def to_next(x, step):
    size = lax.axis_size("tensor")
    return lax.ppermute(x, "tensor", [(i, (i + step) % size) for i in range(size)])


def relative(x, axis):
    me = lax.axis_index("dp") % INNER
    return jnp.concatenate([lax.dynamic_slice_in_dim(x, me ^ apart, 1, axis) for apart in APART], axis)


def owner(core, step, me_ref):
    return me_ref[0] ^ (core | ((step % 2) << 1) | ((step // 2) << 2))


def heads_kernel(me_ref, near_a_ref, near_b_ref, *refs):
    parts, out_ref = (refs[:4], refs[4:8]), refs[8]
    kinds, places, heads = out_ref.shape[:3]
    sub = near_a_ref.shape[2]

    def block(near_ref, held, kind, at, head):
        if at == 0:
            return near_ref[kind * heads + head, 0]
        rows = pl.ds((kind % 2 * heads + head) * sub, sub)
        return held[kind // 2][0, at - 1, rows, :]

    for step in range(4):

        @pl.when(pl.program_id(0) == step)
        def _():
            own, other = [(held[step // 2], held[2 + step % 2]) for held in parts]
            for kind in range(kinds):
                for at in range(places):
                    for head in range(heads):
                        pair = [
                            block(near_a_ref, own, kind, at, head),
                            block(near_b_ref, other, kind, at, head),
                        ]
                        out_ref[kind, at, head, 0] = jnp.concatenate(pair, 0).astype(BF16)


def part_specs(parts):
    by_x = pl.BlockSpec((1,) + parts[0].shape[1:], lambda k, me_ref: (k % 2, 0, 0, 0))
    by_y = pl.BlockSpec((1,) + parts[2].shape[1:], lambda k, me_ref: (k // 2, 0, 0, 0))
    return [by_x, by_x, by_y, by_y]


def heads_together(me, near, own, other):
    count, _, sub, width = near.shape
    heads = count // 4
    near_spec = lambda core: pl.BlockSpec(
        (count, 1, sub, width), lambda k, me_ref: (0, owner(core, k, me_ref), 0, 0)
    )
    full = pl.pallas_call(
        heads_kernel,
        grid_spec=pltpu.PrefetchScalarGridSpec(
            num_scalar_prefetch=1,
            grid=(4,),
            in_specs=[near_spec(0), near_spec(1)] + part_specs(own) + part_specs(other),
            out_specs=pl.BlockSpec((4, 4, heads, 1, 2 * sub, width), lambda k, me_ref: (0, 0, 0, k, 0, 0)),
        ),
        out_shape=jax.ShapeDtypeStruct((4, 4, heads, 4, 2 * sub, width), BF16),
        compiler_params=pltpu.CompilerParams(vmem_limit_bytes=48 * 2**20),
    )(me, near, near, *own, *other)
    return full.reshape(4, 4 * heads * INNER * sub, width)


def units_kernel(me_ref, near_ref, a_ref, a_far_ref, b_ref, b_far_ref, out_ref):
    step = pl.program_id(0)
    half = a_ref.shape[2]
    out_ref[0, 0] = near_ref[0]

    @pl.when(step < 2)
    def _():
        out_ref[0, 1:, :half] = a_ref[0].astype(BF16)

    @pl.when(step >= 2)
    def _():
        out_ref[0, 1:, :half] = a_far_ref[0].astype(BF16)

    @pl.when(step % 2 == 0)
    def _():
        out_ref[0, 1:, half:] = b_ref[0].astype(BF16)

    @pl.when(step % 2 == 1)
    def _():
        out_ref[0, 1:, half:] = b_far_ref[0].astype(BF16)


def units_together(me, near, core, parts):
    count, width = near.shape[1:]
    full = pl.pallas_call(
        units_kernel,
        grid_spec=pltpu.PrefetchScalarGridSpec(
            num_scalar_prefetch=1,
            grid=(4,),
            in_specs=[pl.BlockSpec((1, count, width), lambda k, me_ref: (owner(core, k, me_ref), 0, 0))]
            + part_specs(parts),
            out_specs=pl.BlockSpec((1, 4, count, width), lambda k, me_ref: (k, 0, 0, 0)),
        ),
        out_shape=jax.ShapeDtypeStruct((4, 4, count, width), BF16),
        compiler_params=pltpu.CompilerParams(vmem_limit_bytes=48 * 2**20),
    )(me, near, *parts)
    return full.reshape(16 * count, width)


def gather_halves(piece, half):
    places = [from_next(piece, step) for step in (1, 2, 3)]
    return [jnp.stack([place[:half] for place in places]), jnp.stack([place[half:] for place in places])]


def both_first(places, recv=lambda x: x):
    return [jnp.stack([held, recv(flip(held, bit))]) for held, bit in zip(places, (1, 2))]


def both_second(held, recv=lambda x: x):
    return [held[0], recv(flip(held[0], 2)), held[1], recv(flip(held[1], 1))]


def scatter_first(held, route, recv=lambda x: x):
    if route:
        got = recv(flip(held[:, 1], 1))
        return held[0, 0] + got[0], held[1, 0] + got[1]
    got = recv(flip(held[1], 2))
    return held[0, 0] + got[0], held[0, 1] + got[1]


def scatter_second(parts, route, recv=lambda x: x):
    return parts[0] + recv(flip(parts[1], 2 if route else 1))


def scatter_place(total, places, step, recv=lambda x: x):
    return places[step] + recv(to_next(total, 1))


def scatter_outer(total):
    bit = BITS
    while (1 << bit) < lax.axis_size("dp"):
        total = total + flip(total, bit)
        bit += 1
    return total


class GatherInOrder:
    def __init__(self, piece):
        self.held, self.bits = piece[None], []

    def hop(self, bit, *others):
        got = flip(self.held, bit)
        self.held = jnp.concatenate([self.held, after(got, others) if others else got], 0)
        self.bits.append(bit)

    def result(self):
        me = lax.axis_index("dp") % INNER
        blocks = []
        for index in range(INNER):
            apart = me ^ index
            place = sum(((apart >> bit) & 1) << at for at, bit in enumerate(self.bits))
            blocks.append(lax.dynamic_index_in_dim(self.held, place, 0))
        return jnp.concatenate(blocks, 0)


class SumEverywhere:
    def __init__(self, x):
        self.total = x

    def hop(self, axis, bit):
        pairs = [(i, i ^ (1 << bit)) for i in range(lax.axis_size(axis))]
        self.total = self.total + lax.ppermute(self.total, axis, pairs)


CHUNK = 512


def lane_masks(width):
    lane = lax.broadcasted_iota(jnp.int32, (1, width), 1)
    return [(lane >= start) & (lane < start + HD) for start in range(0, width, HD)]


def keep(mask, x):
    return jnp.where(mask, x, jnp.zeros_like(x))


def forward_kernel(length_ref, q_ref, k_ref, v_ref, mixed_ref, log_ref):
    keys = k_ref.shape[0]
    valid = lax.broadcasted_iota(jnp.int32, (keys, 1), 0) < length_ref[0]
    masks = lane_masks(q_ref.shape[1])
    turned = v_ref[...].T
    for start in range(0, q_ref.shape[0], CHUNK):
        rows = pl.ds(start, CHUNK)
        for head, mask in enumerate(masks):
            scores = jnp.where(valid, nt(k_ref[...], keep(mask, q_ref[rows, :])), MASKED)
            highest = jnp.max(scores, 0, keepdims=True)
            expo = jnp.exp(scores - highest)
            totals = jnp.sum(expo, 0, keepdims=True)
            log_ref[0, head : head + 1, rows] = highest + jnp.log(totals)
            probs = (expo * (1.0 / totals)).astype(BF16)
            own = slice(head * HD, (head + 1) * HD)
            mixed_ref[own, rows] = nn(turned[own, :], probs).astype(BF16)


def backward_kernel(
    scalars_ref,
    q_ref,
    k_ref,
    v_ref,
    dm_ref,
    log_ref,
    mixed_ref,
    wq_ref,
    wk_ref,
    wv_ref,
    own_ref,
    seq_ref,
    da_ref,
    first_ref,
    near_ref,
    far_ref,
    sums_ref,
    seq_part_ref,
    own_part_ref,
    dk_sum,
    dv_sum,
    dq_all,
    dq_turned,
):
    keys = k_ref.shape[0]
    queries = q_ref.shape[0]
    step = pl.program_id(0)
    valid = lax.broadcasted_iota(jnp.int32, (keys, 1), 0) < scalars_ref[0]
    masks = lane_masks(q_ref.shape[1])
    turned = k_ref[...].T
    for start in range(0, queries, CHUNK):
        rows = pl.ds(start, CHUNK)
        parts = []
        for head, mask in enumerate(masks):
            query = keep(mask, q_ref[rows, :])
            d_mixed = keep(mask, dm_ref[rows, :])
            scores = jnp.where(valid, nt(k_ref[...], query), MASKED)
            probs = jnp.exp(scores - log_ref[0, head : head + 1, rows])
            d_values = nn(probs.astype(BF16), d_mixed)
            d_probs = nt(v_ref[...], d_mixed)
            row_dot = jnp.sum(d_probs * probs, 0, keepdims=True)
            d_scores = (probs * (d_probs - row_dot)).astype(BF16)
            d_keys = nn(d_scores, query)
            parts.append(nn(turned[head * HD : (head + 1) * HD, :], d_scores))
            if start == 0 and head == 0:
                dk_sum[...] = d_keys
                dv_sum[...] = d_values
            else:
                dk_sum[...] += d_keys
                dv_sum[...] += d_values
        part = jnp.concatenate(parts, 0) * HD ** (-0.5)
        dq_turned[:, rows] = part.astype(BF16)
        dq_all[rows, :] = part.T.astype(BF16)
    d_queries = dq_all[...]
    d_keys = dk_sum[...].astype(BF16)
    d_values = dv_sum[...].astype(BF16)
    keys_turned, values_turned = d_keys.T, d_values.T
    sums_ref[0, 0:1] = jnp.sum(d_queries.astype(F32), 0, keepdims=True)
    sums_ref[0, 1:2] = jnp.sum(d_values.astype(F32), 0, keepdims=True)

    sub = HD // INNER
    heads = near_ref.shape[2] // (4 * sub)
    grads = [
        nn(dq_turned[...], own_ref[...]),
        nn(keys_turned, seq_ref[...]),
        nn(values_turned, seq_ref[...]),
        nn(mixed_ref[...], da_ref[...]),
    ]
    for which in range(2):
        head = 2 * step + which
        place = head // heads
        for kind, grad in enumerate(grads):
            rows = pl.ds(pl.multiple_of((kind * heads + head % heads) * sub, sub), sub)
            for block in range(INNER):
                target = far_ref if block % 2 else near_ref
                at = which * HD + block * sub
                target[block // 2, place, rows, :] = grad[at : at + sub, :]

    own_part = tn(wq_ref[...], dq_turned[...])
    seq_part = tn(wk_ref[...], keys_turned) + tn(wv_ref[...], values_turned)

    @pl.when(step == 0)
    def _():
        own_part_ref[...] = own_part + first_ref[...].T
        seq_part_ref[...] = seq_part

    @pl.when(step > 0)
    def _():
        own_part_ref[...] += own_part
        seq_part_ref[...] += seq_part

    @pl.when(step == pl.num_programs(0) - 1)
    def _():
        own = pl.ds(pl.multiple_of(scalars_ref[1], CHUNK), queries)
        seq_part_ref[:, own] += own_part_ref[...]


def attention_forward(length, queries, keys, values):
    count, width = queries.shape
    columns = lambda array: pl.BlockSpec((array.shape[0], 2 * HD), lambda j: (0, j))
    return pl.pallas_call(
        forward_kernel,
        grid=(width // (2 * HD),),
        in_specs=[pl.BlockSpec(memory_space=pltpu.SMEM)]
        + [columns(array) for array in (queries, keys, values)],
        out_specs=[pl.BlockSpec((2 * HD, count), lambda j: (j, 0)), pl.BlockSpec((1, 2, count), lambda j: (j, 0, 0))],
        out_shape=[
            jax.ShapeDtypeStruct((width, count), BF16),
            jax.ShapeDtypeStruct((width // (2 * HD), 2, count), F32),
        ],
        compiler_params=pltpu.CompilerParams(vmem_limit_bytes=48 * 2**20),
        cost_estimate=pl.CostEstimate(flops=count * width, bytes_accessed=2**20, transcendentals=0),
    )(length, queries, keys, values)


def attention_backward(scalars, in_pairs, weights, whole):
    queries, keys, values, d_mixed, logs, mixed = in_pairs
    count, width = queries.shape
    long = keys.shape[0]
    pairs = width // (2 * HD)
    columns = lambda array: pl.BlockSpec((array.shape[0], 2 * HD), lambda j: (0, j))
    of_rows = lambda array: pl.BlockSpec((2 * HD, array.shape[1]), lambda j: (j, 0))
    full = lambda array: pl.BlockSpec(array.shape, lambda j: (0,) * len(array.shape))
    sent = jax.ShapeDtypeStruct((INNER // 2, 4, width // INNER, width), F32)
    part = jax.ShapeDtypeStruct((width, long), F32)
    return pl.pallas_call(
        backward_kernel,
        grid=(pairs,),
        in_specs=[pl.BlockSpec(memory_space=pltpu.SMEM)]
        + [columns(array) for array in (queries, keys, values, d_mixed)]
        + [pl.BlockSpec((1, 2, count), lambda j: (j, 0, 0))]
        + [of_rows(array) for array in (mixed, *weights)]
        + [full(array) for array in whole],
        out_specs=[full(sent), full(sent), pl.BlockSpec((1, 2, 2 * HD), lambda j: (j, 0, 0)), full(part)],
        out_shape=[sent, sent, jax.ShapeDtypeStruct((pairs, 2, 2 * HD), F32), part],
        scratch_shapes=[
            pltpu.VMEM((width, count), F32),
            pltpu.VMEM((long, 2 * HD), F32),
            pltpu.VMEM((long, 2 * HD), F32),
            pltpu.VMEM((count, 2 * HD), BF16),
            pltpu.VMEM((2 * HD, count), BF16),
        ],
        compiler_params=pltpu.CompilerParams(vmem_limit_bytes=56 * 2**20),
        cost_estimate=pl.CostEstimate(flops=count * width, bytes_accessed=2**20, transcendentals=0),
    )(scalars, queries, keys, values, d_mixed, logs, mixed, *weights, *whole)


class ShareInputs:
    def __init__(self, part):
        quarters = part.reshape((4, part.shape[0] // 4, part.shape[1]))
        place = lax.axis_index("tensor")
        self.flipped = place >= 2
        end = jnp.where(self.flipped, 3, 0)
        near = lambda i: lax.dynamic_index_in_dim(quarters, jnp.abs(end - i), 0, keepdims=False)
        self.near = [near(i) for i in range(4)]
        self.outer = (place == 0) | (place == 3)
        swap = [(0, 1), (1, 0), (2, 3), (3, 2)]
        self.first = lax.ppermute(near(jnp.where(self.outer, 3, 0)), "tensor", swap)
        self.second = lax.ppermute(self.near[2], "tensor", [(0, 1), (3, 2)])

    def inner(self):
        self.far_sum, self.across_sum = self.near[3] + self.first, self.near[2] + self.second

    def outward(self, others):
        across = [(1, 2), (2, 1)]
        far = lax.ppermute(after(self.far_sum, others), "tensor", across)
        self.third = lax.ppermute(after(self.near[1], others), "tensor", [(0, 1), (3, 2)])
        self.last = lax.ppermute(far, "tensor", [(2, 3), (1, 0)])
        self.across = lax.ppermute(after(self.across_sum, far), "tensor", across)

    def result(self):
        mine = jnp.where(self.outer, self.near[0] + self.first, self.near[1] + self.third)
        theirs = jnp.where(self.outer, self.last, self.across)
        return jnp.concatenate(
            [jnp.where(self.flipped, theirs, mine), jnp.where(self.flipped, mine, theirs)], 1
        )


def on_device(
    tokens,
    lengths,
    cotangent,
    qkv_weight,
    qv_bias,
    out_weight,
    out_bias,
    first_gain,
    first_shift,
    up_weight,
    up_bias,
    down_weight,
    down_bias,
    second_gain,
    second_shift,
):
    rows, width = tokens.shape
    seq = rows // lengths.shape[0]
    columns = qkv_weight.shape[2]
    heads = columns // HD
    units = up_weight.shape[1]
    share = rows // 4
    sub = HD // INNER
    count = units // INNER
    scale = jnp.asarray(HD ** (-0.5), BF16)
    place = lax.axis_index("tensor")
    me = lax.axis_index("dp") % INNER
    one = unit(lengths)

    few = heads * sub
    all_heads = jnp.concatenate([qkv_weight.transpose(0, 2, 1), out_weight[None]]).astype(F32) * one
    all_heads = all_heads.reshape(4 * heads, INNER, sub, width)
    qv_heads = qv_bias.reshape(2, heads, INNER, sub)
    up_turned = up_weight.T.reshape(INNER, count, width)
    down_blocks = down_weight.reshape(INNER, count, width)
    up_bias_blocks = up_bias.reshape(INNER, count)
    mine = lambda x, axis: lax.dynamic_index_in_dim(x, me, axis, keepdims=False)
    vectors = jnp.concatenate([mine(up_bias_blocks, 0), mine(qv_heads, 2).reshape(-1)])
    heads_piece = mine(all_heads, 1).reshape(4 * few, width)
    vector_rows = jnp.pad(vectors[None], ((0, 7), (0, width - vectors.shape[0])))
    heads_piece = jnp.concatenate([heads_piece[: 2 * few], vector_rows, heads_piece[2 * few :]])
    up_piece = mine(up_turned, 0).astype(F32) * one
    down_piece = mine(down_blocks, 0).astype(F32) * one

    heads_places = gather_halves(heads_piece, 2 * few + 8)
    heads_first = both_first(heads_places)
    up_places = gather_halves(after(up_piece, heads_places), count // 2)
    heads_far = both_second(heads_first)
    heads_other = [flip(part, 0) for part in heads_far]

    spot = (slice(None), slice(None), 2 * few, slice(vectors.shape[0]))
    small_far = jnp.stack([jnp.stack([part[spot] for part in far[:2]]) for far in (heads_far, heads_other)])
    up_bias_near = relative(up_bias_blocks, 0).reshape(2, 2, 2, 1, count)
    up_bias_full = jnp.concatenate([up_bias_near, small_far[..., :count]], 3).reshape(2, 2 * units)
    qv_far = small_far[..., count:].reshape(2, 2, 2, 3, 2, heads, sub)
    qv_near = relative(qv_heads, 2).reshape(2, heads, 2, 2, 2, sub).transpose(0, 1, 3, 4, 2, 5)
    qv_full = [qv_near.reshape(2, columns), qv_far.transpose(4, 3, 5, 1, 2, 0, 6).reshape(2, 3 * columns)]
    qv_full = jnp.concatenate(qv_full, 1)

    def heads_apart(array, places):
        trail = array.shape[1:]
        both = array.reshape((places, heads, 2, 2, 2, sub) + trail)
        both = both.transpose((4, 2, 3, 0, 1, 5) + tuple(range(6, 6 + len(trail))))
        return both.reshape((2, 2, 2, places, few) + trail)

    which = place // 2
    length = lax.dynamic_slice_in_dim(lengths, which, 1, 0)
    seq_tokens = lax.dynamic_slice_in_dim(tokens, which * seq, seq, 0)
    own_tokens = lax.dynamic_slice_in_dim(tokens, place * share, share, 0)
    own_cotangent = lax.dynamic_slice_in_dim(cotangent, place * share, share, 0)
    whole_heads = heads_together(me[None], all_heads, heads_far, heads_other)
    down_places = gather_halves(after(down_piece, up_places, whole_heads), count // 2)
    up_first = both_first(after(up_places, heads_far), lambda x: after(x, whole_heads))
    q_rows, k_rows, v_rows, out_rows = after(whole_heads, up_first)
    queries = (nt(own_tokens, q_rows) + qv_full[0]).astype(BF16) * scale
    keys = nt(seq_tokens, k_rows).astype(BF16)
    values = (nt(seq_tokens, v_rows) + qv_full[1]).astype(BF16)
    turned_mixed, logs = attention_forward(length, after(queries, down_places, keys, values), keys, values)
    late = lambda x: after(x, turned_mixed)
    up_far = both_second(up_first, late)
    down_first = both_first(after(down_places, up_first), late)
    turned_mixed = after(turned_mixed, up_far, down_first)
    up_other = [flip(part, 0) for part in up_far]
    first = own_tokens.astype(F32) + (tn(turned_mixed, out_rows) + out_bias)
    normed, first_back = jax.vjp(layer_norm, first, first_gain, first_shift)
    normed_low = normed.astype(BF16)

    up_full = [units_together(me[None], up_turned, core, parts) for core, parts in enumerate((up_far, up_other))]
    hidden, active, gelu_back = [], [], []
    down_far = None
    for core in range(2):
        hidden.append(nt(normed_low, up_full[core]) + up_bias_full[core])
        value, back = jax.vjp(exact_gelu, hidden[core])
        active.append(value.astype(BF16))
        gelu_back.append(back)
        if core == 0:
            down_far = both_second(down_first, lambda x: after(x, active[0]))
        normed_low = after(normed_low, active[core], down_far)
    down_other = [flip(part, 0) for part in down_far]
    down_full = [units_together(me[None], down_blocks, 0, down_far)]
    branch = nn(after(active[0], active[1]), down_full[0])
    down_full.append(units_together(me[None], down_blocks, 1, after(down_other, branch)))
    branch = branch + nn(active[1], down_full[1])
    second = normed + (branch + down_bias)
    result, second_back = jax.vjp(layer_norm, second, second_gain, second_shift)
    gathered = lax.all_gather(result, "tensor", axis=0, tiled=True)

    d_second, grad_second_gain, grad_second_shift = second_back(own_cotangent.astype(F32))
    d_branch = d_second.astype(BF16)
    grad_down_bias = jnp.sum(d_branch.astype(F32), 0)

    blocks = (2, 2, 4, count, width)
    down_sent = tn(active[1], d_branch)
    d_branch = after(d_branch, down_sent)
    d_hidden = [None, gelu_back[1](nt(d_branch, down_full[1]))[0].astype(BF16)]
    up_sent = tn(d_hidden[1], normed_low)
    d_branch = after(d_branch, up_sent)
    d_hidden[0] = gelu_back[0](nt(d_branch, down_full[0]))[0].astype(BF16)
    down_held = (tn(active[0], after(d_branch, d_hidden[0])) + flip(down_sent, 0)).reshape(blocks)
    up_held = (tn(d_hidden[0], after(normed_low, down_held)) + flip(up_sent, 0)).reshape(blocks)
    d_hidden = after(d_hidden, up_held)
    d_normed = nn(d_hidden[0], up_full[0]) + nn(d_hidden[1], up_full[1]) + d_second
    grad_up_bias = jnp.concatenate([jnp.sum(part.astype(F32), 0) for part in d_hidden])
    d_first, grad_first_gain, grad_first_shift = first_back(d_normed)
    d_attended = d_first.astype(BF16)
    grad_out_bias = jnp.sum(d_attended.astype(F32), 0)
    d_mixed = nt(d_attended, out_rows).astype(BF16)

    d_mixed = after(d_mixed, up_held)
    scalars = jnp.concatenate([length, ((place % 2) * share)[None]])
    near, far, column_sums, input_part = attention_backward(
        scalars,
        (queries, keys, values, d_mixed, logs, turned_mixed),
        (q_rows, k_rows, v_rows),
        (own_tokens, seq_tokens, d_attended, d_first),
    )

    late = lambda x: after(x, input_part)
    down_held = scatter_first(down_held, 0, late)
    up_held = scatter_first(up_held, 1, late)
    near, far, column_sums, input_part = after(
        (near, far, column_sums, input_part), down_held, up_held
    )
    output = (gathered * one).astype(BF16)
    got = flip(far, 0)
    cut = lambda array, half: array[:, 2 * half : 2 * half + 2].reshape((2, 2, 2) + array.shape[2:])
    attn_held = [cut(near, half) + cut(got, half) for half in range(2)]
    attn_sent = attn_held
    share_inputs = ShareInputs(input_part)
    late = lambda x: after(x, attn_held)
    down_held = scatter_second(down_held, 0, late)
    up_held = scatter_second(up_held, 1, late)
    mlp_places = jnp.concatenate([up_held, down_held], 1)
    share_inputs.inner()
    late = lambda x: after(x, share_inputs.far_sum, share_inputs.across_sum, gathered)
    mlp_sums = scatter_place(mlp_places[3], mlp_places, 2, late)
    late = lambda x: after(x, mlp_sums)
    attn_held = [scatter_first(held, half, late) for half, held in enumerate(attn_held)]
    mlp_sums = scatter_place(mlp_sums, mlp_places, 1, lambda x: after(x, attn_held))
    attn_held = [scatter_second(held, half) for half, held in enumerate(attn_held)]
    attn_places = [held[i] for held in attn_held for i in range(2)]
    mlp_sums = scatter_place(mlp_sums, mlp_places, 0, lambda x: after(x, attn_places))
    attn_sums = attn_places[3]
    for step in (2, 1, 0):
        attn_sums = scatter_place(attn_sums, attn_places, step)
    mlp_sums, attn_sums = scatter_outer(mlp_sums), scatter_outer(attn_sums)
    up_gather, down_gather = [GatherInOrder(mlp_sums[i * count : (i + 1) * count]) for i in (0, 1)]
    up_gather.hop(1)
    down_gather.hop(2)
    attn_gather = GatherInOrder(attn_sums)
    qv_sums = column_sums.transpose(0, 2, 1).reshape(width, 2)
    qv_sums = heads_apart(qv_sums, 4).transpose(0, 1, 2, 3, 5, 4).reshape(4 * INNER, 2 * few)
    vector_blocks = jnp.concatenate([grad_up_bias.reshape(4 * INNER, count), qv_sums], 1)
    index = jnp.arange(4 * INNER, dtype=jnp.int32)
    apart = (index % INNER) ^ me
    step = (index // INNER + 4 - place) % 4
    order = (apart & 1) * 16 + (apart >> 2) * 8 + ((apart >> 1) & 1) * 4 + step
    vector_blocks = jnp.take(vector_blocks, order, axis=0)
    vectors = [
        grad_out_bias,
        grad_first_gain,
        grad_first_shift,
        grad_down_bias,
        grad_second_gain,
        grad_second_shift,
    ]
    small = jnp.concatenate([vector_blocks.reshape(-1), *vectors]).reshape(-1, 128)
    small = SumEverywhere(after(small, attn_sums))
    small.hop("dp", 0)
    up_gather.hop(2)
    down_gather.hop(1)
    attn_gather.hop(2, small.total)
    small.hop("tensor", 0)
    small.hop("tensor", 1)
    share_inputs.outward(small.total)
    up_gather.hop(0)
    down_gather.hop(0)
    attn_gather.hop(1, small.total, up_gather.held, down_gather.held)
    grad_tokens = share_inputs.result().T
    for bit in range(1, lax.axis_size("dp").bit_length() - 1):
        small.hop("dp", bit)
    small = small.total.reshape(-1)
    grad_up = up_gather.result().reshape(units, width).T
    grad_down = down_gather.result().reshape(units, width)
    attn_gather.hop(0, output, grad_up, grad_down)
    attn_all = attn_gather.result()
    attn_all = attn_all.reshape(INNER, 4, heads, sub, width).transpose(1, 2, 0, 3, 4)
    attn_all = attn_all.reshape(4, columns, width)

    blocks = small[: vector_blocks.size].reshape(4, INNER, -1)
    blocks = lax.dynamic_index_in_dim(blocks, place, 0, keepdims=False)
    qv_all = blocks[:, count:].reshape(INNER, 2, heads, sub)
    small = small[small.size - 6 * width :].reshape(6, width)
    return (
        output,
        grad_tokens,
        attn_all[:3].transpose(0, 2, 1),
        qv_all.transpose(1, 2, 0, 3).reshape(2, columns),
        attn_all[3],
        small[0],
        small[1],
        small[2],
        grad_up,
        blocks[:, :count].reshape(-1),
        grad_down,
        small[3],
        small[4],
        small[5],
    )


def solution(mesh):
    placed = (
        P("dp", None),
        P("dp"),
        P("dp", None),
        P(None, None, "tensor"),
        P(None, "tensor"),
        P("tensor", None),
        P(),
        P(),
        P(),
        P(None, "tensor"),
        P("tensor"),
        P("tensor", None),
        P(),
        P(),
        P(),
    )
    return jax.shard_map(
        on_device,
        mesh=mesh,
        in_specs=placed,
        out_specs=(
            P("dp", None),
            P("dp", "tensor"),
            P(None, None, "tensor"),
            P(None, "tensor"),
            P("tensor", None),
            P(),
            P(),
            P(),
            P(None, "tensor"),
            P("tensor"),
            P("tensor", None),
            P(),
            P(),
            P(),
        ),
        check_vma=False,
    )
```

```python
import jax
import jax.numpy as jnp
from jax import lax
from jax.experimental import pallas as pl
from jax.experimental.pallas import tpu as pltpu
from jax.sharding import PartitionSpec as P

HD = 64
EPS = 1e-05
MASKED = -1000000000.0
BITS = 3
INNER = 1 << BITS
F32 = jnp.float32
BF16 = jnp.bfloat16


def layer_norm(hidden, gain, shift):
    center = hidden - jnp.mean(hidden, -1, keepdims=True)
    spread = jnp.mean(center * center, -1, keepdims=True)
    return center * lax.rsqrt(spread + EPS) * gain + shift


def exact_gelu(inputs):
    return jax.nn.gelu(inputs, approximate=False)


def nn(left, right):
    return lax.dot_general(left, right, (((1,), (0,)), ((), ())), preferred_element_type=F32)


def nt(left, right):
    return lax.dot_general(left, right, (((1,), (1,)), ((), ())), preferred_element_type=F32)


def tn(left, right):
    return lax.dot_general(left, right, (((0,), (0,)), ((), ())), preferred_element_type=F32)


APART = [c | (x << 1) | (y << 2) for c in (0, 1) for y in (0, 1) for x in (0, 1)]


def unit(lengths):
    return jnp.where(lengths[0] > 0, 1.0, 0.0).astype(F32)


def after(x, *others):
    return lax.optimization_barrier((x, others))[0]


def flip(x, bit):
    size = lax.axis_size("dp")
    return lax.ppermute(x, "dp", [(i, i ^ (1 << bit)) for i in range(size)])


def from_next(x, step):
    size = lax.axis_size("tensor")
    return lax.ppermute(x, "tensor", [((i + step) % size, i) for i in range(size)])


def to_next(x, step):
    size = lax.axis_size("tensor")
    return lax.ppermute(x, "tensor", [(i, (i + step) % size) for i in range(size)])


def relative(x, axis):
    me = lax.axis_index("dp") % INNER
    return jnp.concatenate([lax.dynamic_slice_in_dim(x, me ^ apart, 1, axis) for apart in APART], axis)


def owner(core, step, me_ref):
    return me_ref[0] ^ (core | ((step % 2) << 1) | ((step // 2) << 2))


def heads_kernel(me_ref, near_a_ref, near_b_ref, *refs):
    parts, out_ref = (refs[:4], refs[4:8]), refs[8]
    kinds, places, heads = out_ref.shape[:3]
    sub = near_a_ref.shape[2]

    def block(near_ref, held, kind, at, head):
        if at == 0:
            return near_ref[kind * heads + head, 0]
        rows = pl.ds((kind % 2 * heads + head) * sub, sub)
        return held[kind // 2][0, at - 1, rows, :]

    for step in range(4):

        @pl.when(pl.program_id(0) == step)
        def _():
            own, other = [(held[step // 2], held[2 + step % 2]) for held in parts]
            for kind in range(kinds):
                for at in range(places):
                    for head in range(heads):
                        pair = [
                            block(near_a_ref, own, kind, at, head),
                            block(near_b_ref, other, kind, at, head),
                        ]
                        out_ref[kind, at, head, 0] = jnp.concatenate(pair, 0).astype(BF16)


def part_specs(parts):
    by_x = pl.BlockSpec((1,) + parts[0].shape[1:], lambda k, me_ref: (k % 2, 0, 0, 0))
    by_y = pl.BlockSpec((1,) + parts[2].shape[1:], lambda k, me_ref: (k // 2, 0, 0, 0))
    return [by_x, by_x, by_y, by_y]


def heads_together(me, near, own, other):
    count, _, sub, width = near.shape
    heads = count // 4
    near_spec = lambda core: pl.BlockSpec(
        (count, 1, sub, width), lambda k, me_ref: (0, owner(core, k, me_ref), 0, 0)
    )
    full = pl.pallas_call(
        heads_kernel,
        grid_spec=pltpu.PrefetchScalarGridSpec(
            num_scalar_prefetch=1,
            grid=(4,),
            in_specs=[near_spec(0), near_spec(1)] + part_specs(own) + part_specs(other),
            out_specs=pl.BlockSpec((4, 4, heads, 1, 2 * sub, width), lambda k, me_ref: (0, 0, 0, k, 0, 0)),
        ),
        out_shape=jax.ShapeDtypeStruct((4, 4, heads, 4, 2 * sub, width), BF16),
        compiler_params=pltpu.CompilerParams(vmem_limit_bytes=48 * 2**20),
    )(me, near, near, *own, *other)
    return full.reshape(4, 4 * heads * INNER * sub, width)


def units_kernel(me_ref, near_ref, a_ref, a_far_ref, b_ref, b_far_ref, out_ref):
    step = pl.program_id(0)
    half = a_ref.shape[2]
    out_ref[0, 0] = near_ref[0]

    @pl.when(step < 2)
    def _():
        out_ref[0, 1:, :half] = a_ref[0].astype(BF16)

    @pl.when(step >= 2)
    def _():
        out_ref[0, 1:, :half] = a_far_ref[0].astype(BF16)

    @pl.when(step % 2 == 0)
    def _():
        out_ref[0, 1:, half:] = b_ref[0].astype(BF16)

    @pl.when(step % 2 == 1)
    def _():
        out_ref[0, 1:, half:] = b_far_ref[0].astype(BF16)


def units_together(me, near, core, parts):
    count, width = near.shape[1:]
    full = pl.pallas_call(
        units_kernel,
        grid_spec=pltpu.PrefetchScalarGridSpec(
            num_scalar_prefetch=1,
            grid=(4,),
            in_specs=[pl.BlockSpec((1, count, width), lambda k, me_ref: (owner(core, k, me_ref), 0, 0))]
            + part_specs(parts),
            out_specs=pl.BlockSpec((1, 4, count, width), lambda k, me_ref: (k, 0, 0, 0)),
        ),
        out_shape=jax.ShapeDtypeStruct((4, 4, count, width), BF16),
        compiler_params=pltpu.CompilerParams(vmem_limit_bytes=48 * 2**20),
    )(me, near, *parts)
    return full.reshape(16 * count, width)


def gather_halves(piece, half):
    places = [from_next(piece, step) for step in (1, 2, 3)]
    return [jnp.stack([place[:half] for place in places]), jnp.stack([place[half:] for place in places])]


def both_first(places, recv=lambda x: x):
    return [jnp.stack([held, recv(flip(held, bit))]) for held, bit in zip(places, (1, 2))]


def both_second(held, recv=lambda x: x):
    return [held[0], recv(flip(held[0], 2)), held[1], recv(flip(held[1], 1))]


def scatter_first(held, route, recv=lambda x: x):
    if route:
        got = recv(flip(held[:, 1], 1))
        return held[0, 0] + got[0], held[1, 0] + got[1]
    got = recv(flip(held[1], 2))
    return held[0, 0] + got[0], held[0, 1] + got[1]


def scatter_second(parts, route, recv=lambda x: x):
    return parts[0] + recv(flip(parts[1], 2 if route else 1))


def scatter_place(total, places, step, recv=lambda x: x):
    return places[step] + recv(to_next(total, 1))


def scatter_outer(total):
    bit = BITS
    while (1 << bit) < lax.axis_size("dp"):
        total = total + flip(total, bit)
        bit += 1
    return total


class GatherInOrder:
    def __init__(self, piece):
        self.held, self.bits = piece[None], []

    def hop(self, bit, *others):
        got = flip(self.held, bit)
        self.held = jnp.concatenate([self.held, after(got, others) if others else got], 0)
        self.bits.append(bit)

    def result(self):
        me = lax.axis_index("dp") % INNER
        blocks = []
        for index in range(INNER):
            apart = me ^ index
            place = sum(((apart >> bit) & 1) << at for at, bit in enumerate(self.bits))
            blocks.append(lax.dynamic_index_in_dim(self.held, place, 0))
        return jnp.concatenate(blocks, 0)


class SumEverywhere:
    def __init__(self, x):
        self.total = x

    def hop(self, axis, bit):
        pairs = [(i, i ^ (1 << bit)) for i in range(lax.axis_size(axis))]
        self.total = self.total + lax.ppermute(self.total, axis, pairs)


CHUNK = 512


def lane_masks(width):
    lane = lax.broadcasted_iota(jnp.int32, (1, width), 1)
    return [(lane >= start) & (lane < start + HD) for start in range(0, width, HD)]


def keep(mask, x):
    return jnp.where(mask, x, jnp.zeros_like(x))


def forward_kernel(length_ref, q_ref, k_ref, v_ref, mixed_ref, log_ref):
    keys = k_ref.shape[0]
    valid = lax.broadcasted_iota(jnp.int32, (keys, 1), 0) < length_ref[0]
    masks = lane_masks(q_ref.shape[1])
    turned = v_ref[...].T
    for start in range(0, q_ref.shape[0], CHUNK):
        rows = pl.ds(start, CHUNK)
        for head, mask in enumerate(masks):
            scores = jnp.where(valid, nt(k_ref[...], keep(mask, q_ref[rows, :])), MASKED)
            highest = jnp.max(scores, 0, keepdims=True)
            expo = jnp.exp(scores - highest)
            totals = jnp.sum(expo, 0, keepdims=True)
            log_ref[0, head : head + 1, rows] = highest + jnp.log(totals)
            probs = (expo * (1.0 / totals)).astype(BF16)
            own = slice(head * HD, (head + 1) * HD)
            mixed_ref[own, rows] = nn(turned[own, :], probs).astype(BF16)


def backward_kernel(
    scalars_ref,
    q_ref,
    k_ref,
    v_ref,
    dm_ref,
    log_ref,
    mixed_ref,
    wq_ref,
    wk_ref,
    wv_ref,
    own_ref,
    seq_ref,
    da_ref,
    first_ref,
    near_ref,
    far_ref,
    sums_ref,
    seq_part_ref,
    own_part_ref,
    dk_sum,
    dv_sum,
    dq_all,
    dq_turned,
):
    keys = k_ref.shape[0]
    queries = q_ref.shape[0]
    step = pl.program_id(0)
    valid = lax.broadcasted_iota(jnp.int32, (keys, 1), 0) < scalars_ref[0]
    masks = lane_masks(q_ref.shape[1])
    turned = k_ref[...].T
    for start in range(0, queries, CHUNK):
        rows = pl.ds(start, CHUNK)
        parts = []
        for head, mask in enumerate(masks):
            query = keep(mask, q_ref[rows, :])
            d_mixed = keep(mask, dm_ref[rows, :])
            scores = jnp.where(valid, nt(k_ref[...], query), MASKED)
            probs = jnp.exp(scores - log_ref[0, head : head + 1, rows])
            d_values = nn(probs.astype(BF16), d_mixed)
            d_probs = nt(v_ref[...], d_mixed)
            row_dot = jnp.sum(d_probs * probs, 0, keepdims=True)
            d_scores = (probs * (d_probs - row_dot)).astype(BF16)
            d_keys = nn(d_scores, query)
            parts.append(nn(turned[head * HD : (head + 1) * HD, :], d_scores))
            if start == 0 and head == 0:
                dk_sum[...] = d_keys
                dv_sum[...] = d_values
            else:
                dk_sum[...] += d_keys
                dv_sum[...] += d_values
        part = jnp.concatenate(parts, 0) * HD ** (-0.5)
        dq_turned[:, rows] = part.astype(BF16)
        dq_all[rows, :] = part.T.astype(BF16)
    d_queries = dq_all[...]
    d_keys = dk_sum[...].astype(BF16)
    d_values = dv_sum[...].astype(BF16)
    keys_turned, values_turned = d_keys.T, d_values.T
    sums_ref[0, 0:1] = jnp.sum(d_queries.astype(F32), 0, keepdims=True)
    sums_ref[0, 1:2] = jnp.sum(d_values.astype(F32), 0, keepdims=True)

    sub = HD // INNER
    heads = near_ref.shape[2] // (4 * sub)
    grads = [
        nn(dq_turned[...], own_ref[...]),
        nn(keys_turned, seq_ref[...]),
        nn(values_turned, seq_ref[...]),
        nn(mixed_ref[...], da_ref[...]),
    ]
    for which in range(2):
        head = 2 * step + which
        place = head // heads
        for kind, grad in enumerate(grads):
            rows = pl.ds(pl.multiple_of((kind * heads + head % heads) * sub, sub), sub)
            for block in range(INNER):
                target = far_ref if block % 2 else near_ref
                at = which * HD + block * sub
                target[block // 2, place, rows, :] = grad[at : at + sub, :]

    own_part = tn(wq_ref[...], dq_turned[...])
    seq_part = tn(wk_ref[...], keys_turned) + tn(wv_ref[...], values_turned)

    @pl.when(step == 0)
    def _():
        own_part_ref[...] = own_part + first_ref[...].T
        seq_part_ref[...] = seq_part

    @pl.when(step > 0)
    def _():
        own_part_ref[...] += own_part
        seq_part_ref[...] += seq_part

    @pl.when(step == pl.num_programs(0) - 1)
    def _():
        own = pl.ds(pl.multiple_of(scalars_ref[1], CHUNK), queries)
        seq_part_ref[:, own] += own_part_ref[...]


def attention_forward(length, queries, keys, values):
    count, width = queries.shape
    columns = lambda array: pl.BlockSpec((array.shape[0], 2 * HD), lambda j: (0, j))
    return pl.pallas_call(
        forward_kernel,
        grid=(width // (2 * HD),),
        in_specs=[pl.BlockSpec(memory_space=pltpu.SMEM)]
        + [columns(array) for array in (queries, keys, values)],
        out_specs=[pl.BlockSpec((2 * HD, count), lambda j: (j, 0)), pl.BlockSpec((1, 2, count), lambda j: (j, 0, 0))],
        out_shape=[
            jax.ShapeDtypeStruct((width, count), BF16),
            jax.ShapeDtypeStruct((width // (2 * HD), 2, count), F32),
        ],
        compiler_params=pltpu.CompilerParams(vmem_limit_bytes=48 * 2**20),
        cost_estimate=pl.CostEstimate(flops=count * width, bytes_accessed=2**20, transcendentals=0),
    )(length, queries, keys, values)


def attention_backward(scalars, in_pairs, weights, whole):
    queries, keys, values, d_mixed, logs, mixed = in_pairs
    count, width = queries.shape
    long = keys.shape[0]
    pairs = width // (2 * HD)
    columns = lambda array: pl.BlockSpec((array.shape[0], 2 * HD), lambda j: (0, j))
    of_rows = lambda array: pl.BlockSpec((2 * HD, array.shape[1]), lambda j: (j, 0))
    full = lambda array: pl.BlockSpec(array.shape, lambda j: (0,) * len(array.shape))
    sent = jax.ShapeDtypeStruct((INNER // 2, 4, width // INNER, width), F32)
    part = jax.ShapeDtypeStruct((width, long), F32)
    return pl.pallas_call(
        backward_kernel,
        grid=(pairs,),
        in_specs=[pl.BlockSpec(memory_space=pltpu.SMEM)]
        + [columns(array) for array in (queries, keys, values, d_mixed)]
        + [pl.BlockSpec((1, 2, count), lambda j: (j, 0, 0))]
        + [of_rows(array) for array in (mixed, *weights)]
        + [full(array) for array in whole],
        out_specs=[full(sent), full(sent), pl.BlockSpec((1, 2, 2 * HD), lambda j: (j, 0, 0)), full(part)],
        out_shape=[sent, sent, jax.ShapeDtypeStruct((pairs, 2, 2 * HD), F32), part],
        scratch_shapes=[
            pltpu.VMEM((width, count), F32),
            pltpu.VMEM((long, 2 * HD), F32),
            pltpu.VMEM((long, 2 * HD), F32),
            pltpu.VMEM((count, 2 * HD), BF16),
            pltpu.VMEM((2 * HD, count), BF16),
        ],
        compiler_params=pltpu.CompilerParams(vmem_limit_bytes=56 * 2**20),
        cost_estimate=pl.CostEstimate(flops=count * width, bytes_accessed=2**20, transcendentals=0),
    )(scalars, queries, keys, values, d_mixed, logs, mixed, *weights, *whole)


class ShareInputs:
    def __init__(self, part):
        quarters = part.reshape((4, part.shape[0] // 4, part.shape[1]))
        place = lax.axis_index("tensor")
        self.flipped = place >= 2
        end = jnp.where(self.flipped, 3, 0)
        near = lambda i: lax.dynamic_index_in_dim(quarters, jnp.abs(end - i), 0, keepdims=False)
        self.near = [near(i) for i in range(4)]
        self.outer = (place == 0) | (place == 3)
        swap = [(0, 1), (1, 0), (2, 3), (3, 2)]
        self.first = lax.ppermute(near(jnp.where(self.outer, 3, 0)), "tensor", swap)
        self.second = lax.ppermute(self.near[2], "tensor", [(0, 1), (3, 2)])

    def inner(self):
        self.far_sum, self.across_sum = self.near[3] + self.first, self.near[2] + self.second

    def outward(self, others):
        across = [(1, 2), (2, 1)]
        far = lax.ppermute(after(self.far_sum, others), "tensor", across)
        self.third = lax.ppermute(after(self.near[1], others), "tensor", [(0, 1), (3, 2)])
        self.last = lax.ppermute(far, "tensor", [(2, 3), (1, 0)])
        self.across = lax.ppermute(after(self.across_sum, far), "tensor", across)

    def result(self):
        mine = jnp.where(self.outer, self.near[0] + self.first, self.near[1] + self.third)
        theirs = jnp.where(self.outer, self.last, self.across)
        return jnp.concatenate(
            [jnp.where(self.flipped, theirs, mine), jnp.where(self.flipped, mine, theirs)], 1
        )


def on_device(
    tokens,
    lengths,
    cotangent,
    qkv_weight,
    qv_bias,
    out_weight,
    out_bias,
    first_gain,
    first_shift,
    up_weight,
    up_bias,
    down_weight,
    down_bias,
    second_gain,
    second_shift,
):
    rows, width = tokens.shape
    seq = rows // lengths.shape[0]
    columns = qkv_weight.shape[2]
    heads = columns // HD
    units = up_weight.shape[1]
    share = rows // 4
    sub = HD // INNER
    count = units // INNER
    scale = jnp.asarray(HD ** (-0.5), BF16)
    place = lax.axis_index("tensor")
    me = lax.axis_index("dp") % INNER
    one = unit(lengths)

    few = heads * sub
    all_heads = jnp.concatenate([qkv_weight.transpose(0, 2, 1), out_weight[None]]).astype(F32) * one
    all_heads = all_heads.reshape(4 * heads, INNER, sub, width)
    qv_heads = qv_bias.reshape(2, heads, INNER, sub)
    up_turned = up_weight.T.reshape(INNER, count, width)
    down_blocks = down_weight.reshape(INNER, count, width)
    up_bias_blocks = up_bias.reshape(INNER, count)
    mine = lambda x, axis: lax.dynamic_index_in_dim(x, me, axis, keepdims=False)
    vectors = jnp.concatenate([mine(up_bias_blocks, 0), mine(qv_heads, 2).reshape(-1)])
    heads_piece = mine(all_heads, 1).reshape(4 * few, width)
    vector_rows = jnp.pad(vectors[None], ((0, 7), (0, width - vectors.shape[0])))
    heads_piece = jnp.concatenate([heads_piece[: 2 * few], vector_rows, heads_piece[2 * few :]])
    up_piece = mine(up_turned, 0).astype(F32) * one
    down_piece = mine(down_blocks, 0).astype(F32) * one

    heads_places = gather_halves(heads_piece, 2 * few + 8)
    heads_first = both_first(heads_places, lambda x: after(x, up_piece, down_piece))
    up_places = gather_halves(after(up_piece, heads_places), count // 2)
    heads_far = both_second(heads_first)
    heads_other = [flip(part, 0) for part in heads_far]

    spot = (slice(None), slice(None), 2 * few, slice(vectors.shape[0]))
    small_far = jnp.stack([jnp.stack([part[spot] for part in far[:2]]) for far in (heads_far, heads_other)])
    up_bias_near = relative(up_bias_blocks, 0).reshape(2, 2, 2, 1, count)
    up_bias_full = jnp.concatenate([up_bias_near, small_far[..., :count]], 3).reshape(2, 2 * units)
    qv_far = small_far[..., count:].reshape(2, 2, 2, 3, 2, heads, sub)
    qv_near = relative(qv_heads, 2).reshape(2, heads, 2, 2, 2, sub).transpose(0, 1, 3, 4, 2, 5)
    qv_full = [qv_near.reshape(2, columns), qv_far.transpose(4, 3, 5, 1, 2, 0, 6).reshape(2, 3 * columns)]
    qv_full = jnp.concatenate(qv_full, 1)

    def heads_apart(array, places):
        trail = array.shape[1:]
        both = array.reshape((places, heads, 2, 2, 2, sub) + trail)
        both = both.transpose((4, 2, 3, 0, 1, 5) + tuple(range(6, 6 + len(trail))))
        return both.reshape((2, 2, 2, places, few) + trail)

    which = place // 2
    length = lax.dynamic_slice_in_dim(lengths, which, 1, 0)
    seq_tokens = lax.dynamic_slice_in_dim(tokens, which * seq, seq, 0)
    own_tokens = lax.dynamic_slice_in_dim(tokens, place * share, share, 0)
    own_cotangent = lax.dynamic_slice_in_dim(cotangent, place * share, share, 0)
    whole_heads = heads_together(me[None], all_heads, heads_far, heads_other)
    down_places = gather_halves(after(down_piece, up_places, whole_heads), count // 2)
    up_first = both_first(after(up_places, heads_far), lambda x: after(x, whole_heads))
    q_rows, k_rows, v_rows, out_rows = after(whole_heads, up_first)
    queries = (nt(own_tokens, q_rows) + qv_full[0]).astype(BF16) * scale
    keys = nt(seq_tokens, k_rows).astype(BF16)
    values = (nt(seq_tokens, v_rows) + qv_full[1]).astype(BF16)
    turned_mixed, logs = attention_forward(length, after(queries, down_places, keys, values), keys, values)
    late = lambda x: after(x, turned_mixed)
    up_far = both_second(up_first, late)
    down_first = both_first(after(down_places, up_first), late)
    turned_mixed = after(turned_mixed, up_far, down_first)
    up_other = [flip(part, 0) for part in up_far]
    first = own_tokens.astype(F32) + (tn(turned_mixed, out_rows) + out_bias)
    normed, first_back = jax.vjp(layer_norm, first, first_gain, first_shift)
    normed_low = normed.astype(BF16)

    up_full = [units_together(me[None], up_turned, core, parts) for core, parts in enumerate((up_far, up_other))]
    hidden, active, gelu_back = [], [], []
    down_far = None
    for core in range(2):
        hidden.append(nt(normed_low, up_full[core]) + up_bias_full[core])
        value, back = jax.vjp(exact_gelu, hidden[core])
        active.append(value.astype(BF16))
        gelu_back.append(back)
        if core == 0:
            down_far = both_second(down_first, lambda x: after(x, active[0]))
        normed_low = after(normed_low, active[core], down_far)
    down_other = [flip(part, 0) for part in down_far]
    down_full = [units_together(me[None], down_blocks, 0, down_far)]
    branch = nn(after(active[0], active[1]), down_full[0])
    down_full.append(units_together(me[None], down_blocks, 1, after(down_other, branch)))
    branch = branch + nn(active[1], down_full[1])
    second = normed + (branch + down_bias)
    result, second_back = jax.vjp(layer_norm, second, second_gain, second_shift)
    gathered = lax.all_gather(result, "tensor", axis=0, tiled=True)

    d_second, grad_second_gain, grad_second_shift = second_back(own_cotangent.astype(F32))
    d_branch = d_second.astype(BF16)
    grad_down_bias = jnp.sum(d_branch.astype(F32), 0)

    blocks = (2, 2, 4, count, width)
    down_sent = tn(active[1], d_branch)
    d_branch = after(d_branch, down_sent)
    d_hidden = [None, gelu_back[1](nt(d_branch, down_full[1]))[0].astype(BF16)]
    up_sent = tn(d_hidden[1], normed_low)
    d_branch = after(d_branch, up_sent)
    d_hidden[0] = gelu_back[0](nt(d_branch, down_full[0]))[0].astype(BF16)
    down_held = (tn(active[0], after(d_branch, d_hidden[0])) + flip(down_sent, 0)).reshape(blocks)
    up_held = (tn(d_hidden[0], after(normed_low, down_held)) + flip(up_sent, 0)).reshape(blocks)
    d_hidden = after(d_hidden, up_held)
    d_normed = nn(d_hidden[0], up_full[0]) + nn(d_hidden[1], up_full[1]) + d_second
    grad_up_bias = jnp.concatenate([jnp.sum(part.astype(F32), 0) for part in d_hidden])
    d_first, grad_first_gain, grad_first_shift = first_back(d_normed)
    d_attended = d_first.astype(BF16)
    grad_out_bias = jnp.sum(d_attended.astype(F32), 0)
    d_mixed = nt(d_attended, out_rows).astype(BF16)

    d_mixed = after(d_mixed, up_held)
    scalars = jnp.concatenate([length, ((place % 2) * share)[None]])
    near, far, column_sums, input_part = attention_backward(
        scalars,
        (queries, keys, values, d_mixed, logs, turned_mixed),
        (q_rows, k_rows, v_rows),
        (own_tokens, seq_tokens, d_attended, d_first),
    )

    late = lambda x: after(x, input_part)
    down_held = scatter_first(down_held, 0, late)
    up_held = scatter_first(up_held, 1, late)
    near, far, column_sums, input_part = after(
        (near, far, column_sums, input_part), down_held, up_held
    )
    output = (gathered * one).astype(BF16)
    got = flip(far, 0)
    cut = lambda array, half: array[:, 2 * half : 2 * half + 2].reshape((2, 2, 2) + array.shape[2:])
    attn_held = [cut(near, half) + cut(got, half) for half in range(2)]
    attn_sent = attn_held
    share_inputs = ShareInputs(input_part)
    late = lambda x: after(x, attn_held)
    down_held = scatter_second(down_held, 0, late)
    up_held = scatter_second(up_held, 1, late)
    mlp_places = jnp.concatenate([up_held, down_held], 1)
    share_inputs.inner()
    late = lambda x: after(x, share_inputs.far_sum, share_inputs.across_sum, gathered)
    mlp_sums = scatter_place(mlp_places[3], mlp_places, 2, late)
    late = lambda x: after(x, mlp_sums)
    attn_held = [scatter_first(held, half, late) for half, held in enumerate(attn_held)]
    mlp_sums = scatter_place(mlp_sums, mlp_places, 1, lambda x: after(x, attn_held))
    attn_held = [scatter_second(held, half) for half, held in enumerate(attn_held)]
    attn_places = [held[i] for held in attn_held for i in range(2)]
    mlp_sums = scatter_place(mlp_sums, mlp_places, 0, lambda x: after(x, attn_places))
    attn_sums = attn_places[3]
    for step in (2, 1, 0):
        attn_sums = scatter_place(attn_sums, attn_places, step)
    mlp_sums, attn_sums = scatter_outer(mlp_sums), scatter_outer(attn_sums)
    up_gather, down_gather = [GatherInOrder(mlp_sums[i * count : (i + 1) * count]) for i in (0, 1)]
    up_gather.hop(1)
    down_gather.hop(2)
    attn_gather = GatherInOrder(attn_sums)
    qv_sums = column_sums.transpose(0, 2, 1).reshape(width, 2)
    qv_sums = heads_apart(qv_sums, 4).transpose(0, 1, 2, 3, 5, 4).reshape(4 * INNER, 2 * few)
    vector_blocks = jnp.concatenate([grad_up_bias.reshape(4 * INNER, count), qv_sums], 1)
    index = jnp.arange(4 * INNER, dtype=jnp.int32)
    apart = (index % INNER) ^ me
    step = (index // INNER + 4 - place) % 4
    order = (apart & 1) * 16 + (apart >> 2) * 8 + ((apart >> 1) & 1) * 4 + step
    vector_blocks = jnp.take(vector_blocks, order, axis=0)
    vectors = [
        grad_out_bias,
        grad_first_gain,
        grad_first_shift,
        grad_down_bias,
        grad_second_gain,
        grad_second_shift,
    ]
    small = jnp.concatenate([vector_blocks.reshape(-1), *vectors]).reshape(-1, 128)
    small = SumEverywhere(after(small, attn_sums))
    small.hop("dp", 0)
    up_gather.hop(2)
    down_gather.hop(1)
    attn_gather.hop(2, small.total)
    small.hop("tensor", 0)
    small.hop("tensor", 1)
    share_inputs.outward(small.total)
    up_gather.hop(0)
    down_gather.hop(0)
    attn_gather.hop(1, small.total, up_gather.held, down_gather.held)
    grad_tokens = share_inputs.result().T
    for bit in range(1, lax.axis_size("dp").bit_length() - 1):
        small.hop("dp", bit)
    small = small.total.reshape(-1)
    grad_up = up_gather.result().reshape(units, width).T
    grad_down = down_gather.result().reshape(units, width)
    attn_gather.hop(0, output, grad_up, grad_down)
    attn_all = attn_gather.result()
    attn_all = attn_all.reshape(INNER, 4, heads, sub, width).transpose(1, 2, 0, 3, 4)
    attn_all = attn_all.reshape(4, columns, width)

    blocks = small[: vector_blocks.size].reshape(4, INNER, -1)
    blocks = lax.dynamic_index_in_dim(blocks, place, 0, keepdims=False)
    qv_all = blocks[:, count:].reshape(INNER, 2, heads, sub)
    small = small[small.size - 6 * width :].reshape(6, width)
    return (
        output,
        grad_tokens,
        attn_all[:3].transpose(0, 2, 1),
        qv_all.transpose(1, 2, 0, 3).reshape(2, columns),
        attn_all[3],
        small[0],
        small[1],
        small[2],
        grad_up,
        blocks[:, :count].reshape(-1),
        grad_down,
        small[3],
        small[4],
        small[5],
    )


def solution(mesh):
    placed = (
        P("dp", None),
        P("dp"),
        P("dp", None),
        P(None, None, "tensor"),
        P(None, "tensor"),
        P("tensor", None),
        P(),
        P(),
        P(),
        P(None, "tensor"),
        P("tensor"),
        P("tensor", None),
        P(),
        P(),
        P(),
    )
    return jax.shard_map(
        on_device,
        mesh=mesh,
        in_specs=placed,
        out_specs=(
            P("dp", None),
            P("dp", "tensor"),
            P(None, None, "tensor"),
            P(None, "tensor"),
            P("tensor", None),
            P(),
            P(),
            P(),
            P(None, "tensor"),
            P("tensor"),
            P("tensor", None),
            P(),
            P(),
            P(),
        ),
        check_vma=False,
    )
```
